256 devices in a mesh: rows: 32 (over z, x), cols: 8 (over y, core).
Axes of the slice: x: 4, y: 4, z: 8, core: 2. Of those that a mesh axis runs over, the one named last changes fastest.
Arguments:
- coupling: float32 [2, 16384, 16384], P(None, 'rows', 'cols'), may hold values from -2 to 40, as said below
- initial: float32 [2, 48, 16384], P(None, None, 'rows'), may hold values from -8 to 8
Outputs:
- basis: float32 [2, 48, 16384], P(None, None, ('rows', 'cols'))
- ritz: float32 [4, 2, 48, 48], replicated
The draws below stay inside these ranges and needn't reach their ends.
Inputs may be any that keep to these rules, and one draw needn't show every extreme that they name: `coupling`: H is Hermitian (the first plane symmetric, the second antisymmetric) and positive definite.
All inputs are finite; a program needn't handle non-finite values.
Results may differ from the reference program's by a relative error of at most 0.0003.
Values sent between devices are 32-bit elements; how exact they have to be, the bound alone decides.
A program may use at most 64 MiB of HBM per device.

```python
import jax
import jax.numpy as jnp
from jax import lax

N = 16384
K = 48
ITERS = 4


def draw_coupling(key, part):
    first, second, third, fourth = jax.random.split(jax.random.fold_in(key, 7), 4)
    scales = jax.random.uniform(third, (N,), minval=0.8, maxval=1.25)
    outer = scales[:, None] * scales[None, :]
    shifts = 4.5 + 1.5 * jax.random.uniform(fourth, (N,))
    index = jnp.arange(N, dtype=jnp.int32)
    partner = (index + N // 2) % N
    band = (index[None, :] == partner[:, None]).astype(jnp.float32)
    noise = jax.random.normal(first, (N, N), jnp.float32)
    real_plane = (noise + noise.T) * (0.5 / jnp.sqrt(N * 1.0))
    real_plane = (real_plane + band + jnp.diag(shifts)) * outer
    noise = jax.random.normal(second, (N, N), jnp.float32)
    imag_plane = (noise - noise.T) * (0.5 / jnp.sqrt(N * 1.0)) * outer
    return jnp.stack([real_plane, imag_plane])


def draw_initial(key, part):
    inner = jax.random.fold_in(key, 11)
    position = jnp.arange(N, dtype=jnp.float32) / N
    amplitude = 3.0 ** (0.5 * (position - 0.5))
    values = jnp.clip(jax.random.normal(inner, (2, K, N), jnp.float32), -6.0, 6.0)
    return values * amplitude[None, None, :]


def setup_inputs(seed: int = 0) -> dict:
    key_list = jax.random.split(jax.random.key(seed), 3)
    coupling = draw_coupling(jax.random.fold_in(key_list[2], 71), 0)
    initial = draw_initial(jax.random.fold_in(key_list[2], 71), 0)
    return dict(coupling=coupling, initial=initial)


HIGH = lax.Precision.HIGHEST

def pair_products(left, right):
    real_part = jnp.dot(left[0], right[0].T, precision=HIGH) + jnp.dot(left[1], right[1].T, precision=HIGH)
    imag_part = jnp.dot(left[0], right[1].T, precision=HIGH) - jnp.dot(left[1], right[0].T, precision=HIGH)
    return jnp.stack([real_part, imag_part])

def orthonormal(gram_matrix, images):
    gram_re = gram_matrix[0]
    gram_im = gram_matrix[1]
    vectors = gram_re.shape[0]
    width = images.shape[2]
    upper_pair = jnp.stack([gram_re, -gram_im], axis=-1)
    lower_pair = jnp.stack([gram_im, gram_re], axis=-1)
    embedded = jnp.stack([upper_pair, lower_pair], axis=1).reshape(2 * vectors, 2 * vectors)
    factor = jnp.linalg.cholesky(embedded)
    woven = jnp.transpose(images, (1, 0, 2)).reshape(2 * vectors, width)
    solved = lax.linalg.triangular_solve(factor, woven, left_side=True, lower=True)
    return jnp.transpose(solved.reshape(vectors, 2, width), (1, 0, 2))

def reference(coupling, initial):
    contract = (((1,), (1,)), ((), ()))
    current = initial
    ritz_list = []
    for iteration in range(ITERS):
        stacked = current.reshape(2 * K, N)
        with_real = lax.dot_general(stacked.astype(jnp.float32), coupling[0].astype(jnp.float32), contract, precision=HIGH, preferred_element_type=jnp.float32)
        with_imag = lax.dot_general(stacked.astype(jnp.float32), coupling[1].astype(jnp.float32), contract, precision=HIGH, preferred_element_type=jnp.float32)
        images = jnp.stack([with_real[:K] - with_imag[K:], with_real[K:] + with_imag[:K]])
        gram_matrix = pair_products(images, images) / N
        ritz_list.append(pair_products(current, images) / N)
        current = orthonormal(gram_matrix, images)
    return (current, jnp.stack(ritz_list))
```

```python
import jax
import jax.numpy as jnp
from jax import lax
from jax.experimental import pallas as pl
from jax.experimental.pallas import tpu as pltpu
from jax.sharding import PartitionSpec as P

N = 16384
K = 48
ITERS = 4
X, Z, C = 4, 8, 8
CH = 256
RB = 2 * K // X
F32, BF16 = jnp.float32, jnp.bfloat16
MESH = pl.DeviceIdType.MESH
HIGH = lax.Precision.HIGHEST
NT = (((1,), (1,)), ((), ()))


def dot(a, b, precision=None):
    return jnp.dot(a, b, precision=precision, preferred_element_type=F32)


def dot_nt(a, b, precision=None):
    return lax.dot_general(a, b, NT, precision=precision, preferred_element_type=F32)


def split(value):
    high = value.astype(BF16)
    return high, (value - high.astype(F32)).astype(BF16)


def lanes(shape):
    return lax.broadcasted_iota(jnp.int32, shape, 1)


def turned(packed):
    rolled = pltpu.roll(packed, 64, 1)
    return jnp.where(lanes(packed.shape) < 64, rolled, -rolled)


def stacked_rows(first, second):
    gap = jnp.zeros((64 - K, first.shape[1]), first.dtype)
    return jnp.concatenate([first, gap, second, gap], axis=0)


def gram_packed(left, right):
    return dot_nt(left, stacked_rows(right, turned(right)), HIGH)


def gram_planes(re, im):
    return dot_nt(re, stacked_rows(re, im), HIGH) + dot_nt(im, stacked_rows(im, -re), HIGH)


def planes_of(packed):
    low = lanes(packed.shape) < 64
    return jnp.where(low, packed, 0.0), jnp.where(low, pltpu.roll(packed, 64, 1), 0.0)


def apply_packed(matrix, packed):
    re, im = planes_of(matrix)
    return dot(re[:, :K], packed, HIGH) - dot(im[:, :K], turned(packed), HIGH)


def conj_apply_packed(matrix, packed):
    re, im = planes_of(matrix)
    return dot(re[:, :K], packed, HIGH) + dot(im[:, :K], turned(packed), HIGH)


def embedded(matrix):
    re, im = planes_of(matrix)
    upper = re - pltpu.roll(im, K, 1)
    lower = im + pltpu.roll(re, K, 1)
    return jnp.concatenate([upper, lower], axis=0)[:, : 2 * K]


def inverse_factor(gram):
    lane = lanes((K, 128))
    row = lax.broadcasted_iota(jnp.int32, (K, 128), 0)
    low = lane < 64
    re = jnp.where(low, gram, jnp.where(lane - 64 == row, 1.0, 0.0))
    im = jnp.where(low, pltpu.roll(gram, 64, 1), 0.0)
    done_re, done_im = [], []
    for base in range(0, K, 8):
        below = lax.broadcasted_iota(jnp.int32, (K - base, 1), 0)
        for s in range(8):
            j = base + s
            row_re, row_im = re[s : s + 1], im[s : s + 1]
            inv = 1.0 / re[s : s + 1, j : j + 1]
            m_re = jnp.where(below > s, re[:, j : j + 1] * inv, 0.0)
            m_im = jnp.where(below > s, im[:, j : j + 1] * inv, 0.0)
            re, im = (
                re - (m_re * row_re - m_im * row_im),
                im - (m_re * row_im + m_im * row_re),
            )
        done_re.append(re[:8])
        done_im.append(im[:8])
        re, im = re[8:], im[8:]
    re = jnp.concatenate(done_re, axis=0)
    im = jnp.concatenate(done_im, axis=0)
    pivot = jnp.sum(jnp.where(lane == row, re, 0.0), axis=1, keepdims=True)
    scale = 1.0 / jnp.sqrt(pivot)
    return jnp.where(low, pltpu.roll(re, 64, 1), im) * scale


def pack_pair(re, im):
    low = lanes(re.shape) < 64
    even = jnp.where(low, re, pltpu.roll(im, 64, 1))
    odd = jnp.where(low, pltpu.roll(re, 64, 1), im)
    return even, odd


def unpack_pair(even, odd):
    low = lanes(even.shape) < 64
    re = jnp.where(low, even, pltpu.roll(odd, 64, 1))
    im = jnp.where(low, pltpu.roll(even, 64, 1), odd)
    return re, im


def far_first(k):
    return 4 + (k // 2) * (1 - k % 2) - ((k + 1) // 2) * (k % 2)


def near_first(k):
    return (8 + far_first(7 - k)) % 8


def kernel(coupling, initial, basis, ritz, *scratch):
    (
        stage, hhi, hlo, lhs, part, rsx, red, rsz, gath, ybuf, ysplit, acc, acc2,
        pk, rsy, gy, scat, ypc, gsrc, gyc, gxs, gx, gzs, gz,
        fsrc, fy, fxs, fx, fzs, fz, fall,
        hsem, rsx_s, rsx_r, rsz_s, rsz_r, agz_s, agz_r, agx_s, agx_r,
        rsy_s, rsy_r, agy_s, agy_r, sc_s, sc_r, gyc_s, gyc_r, gx_s, gx_r, gz_s, gz_r,
        fy_s, fy_r, fx_s, fx_r, fz_s, fz_r, fa_s, fa_r,
    ) = scratch
    r, c = lax.axis_index("rows"), lax.axis_index("cols")
    z, x = r // X, r % X

    def at_x(j):
        return (z * X + (x + j) % X, c)

    def at_z(o):
        return (((z + o) % Z) * X + x, c)

    def at_c(k):
        return (r, (c + k) % C)

    def remote(src, dst, send, recv, dev):
        return pltpu.make_async_remote_copy(
            src_ref=src, dst_ref=dst, send_sem=send, recv_sem=recv,
            device_id=dev, device_id_type=MESH,
        )

    def loop(n, f):
        def step(i, carry):
            f(i)
            return carry

        lax.fori_loop(0, n, step, 0)

    def rows_of(j):
        return pl.ds(pl.multiple_of(((x + j) % X) * RB, 8), RB)

    def load(k):
        zc = (z + far_first(k)) % Z
        columns = pl.ds(pl.multiple_of(zc * CH, CH), CH)
        return pltpu.make_async_copy(coupling.at[:, :, columns], stage.at[zc], hsem.at[zc])

    loop(Z, lambda k: load(k).start())

    barrier = pltpu.get_barrier_semaphore()
    partners = [at_x(j) for j in range(1, X)] + [at_z(o) for o in range(1, Z)]
    partners += [at_c(k) for k in range(1, C)]
    for dev in partners:
        pl.semaphore_signal(barrier, inc=1, device_id=dev, device_id_type=MESH)

    def set_left(re, im):
        top = jnp.concatenate([re, im], axis=1)
        bottom = jnp.concatenate([im, -re], axis=1)
        high, low = split(jnp.concatenate([top, bottom], axis=0))
        lhs[...] = jnp.concatenate([high, low], axis=0)

    v_re, v_im = initial[0], initial[1]
    set_left(v_re, v_im)
    for t in range(4):
        even, odd = pack_pair(v_re[:, 128 * t : 128 * t + 128], v_im[:, 128 * t : 128 * t + 128])
        pk[2 * t], pk[2 * t + 1] = even, odd
    v_piece = pk[c]
    pl.semaphore_wait(barrier, len(partners))


    def x_part(j, zc):
        return remote(
            part.at[zc, rows_of(j)], rsx.at[j - 1, zc], rsx_s.at[j - 1, zc], rsx_r.at[j - 1, zc], at_x(j)
        )

    def z_part(o, zc):
        return remote(red.at[zc], rsz.at[o], rsz_s.at[o], rsz_r.at[o], at_z(o))

    def column_product(first):
        def chunk(k):
            zc = (z + far_first(k)) % Z
            if first:
                load(k).wait()
                for t in range(0, 1024, 128):
                    high, low = split(stage[zc, t // 512, t % 512 : t % 512 + 128])
                    hhi[zc, t : t + 128] = high
                    hlo[zc, t : t + 128] = low
            both = dot(lhs[...], hhi[zc])
            rest = dot(lhs[: 2 * K], hlo[zc])
            part[zc] = both[: 2 * K] + both[2 * K :] + rest
            for j in range(1, X):
                x_part(j, zc).start()

        loop(Z, chunk)

    def column_sum():
        def chunk(k):
            o = far_first(k)
            zc = (z + o) % Z
            total = part[zc, rows_of(0)]
            for j in range(1, X):
                x_part(j, zc).wait_recv()
                total = total + rsx[j - 1, zc]
            red[zc] = total

            @pl.when(k < Z - 1)
            def _():
                z_part(o, zc).start()

        loop(Z, chunk)
        total = red[z]
        for o in range(1, Z):
            z_part(o, z).wait_recv()
            total = total + rsz[o]
        return total

    def column_sum_sent():
        def chunk(k):
            o = far_first(k)
            zc = (z + o) % Z
            for j in range(1, X):
                x_part(j, zc).wait_send()

            @pl.when(k < Z - 1)
            def _():
                z_part(o, zc).wait_send()

        loop(Z, chunk)


    def z_whole(o, zc):
        block = gath.at[zc, rows_of(0)]
        return remote(block, block, agz_s.at[o], agz_r.at[o], at_z(o))

    def x_whole(j, zc, shift):
        block = gath.at[zc, rows_of(shift)]
        return remote(block, block, agx_s.at[j - 1, zc], agx_r.at[j - 1, zc], at_x(j))

    def column_gather(total):
        gath[z, rows_of(0)] = total
        loop(Z - 1, lambda k: z_whole(far_first(k), z).start())

        def forward(k):
            o = near_first(k)
            zc = (z + Z - o) % Z

            @pl.when(k > 0)
            def _():
                z_whole(o, zc).wait_recv()

            for j in range(1, X):
                x_whole(j, zc, 0).start()

        loop(Z, forward)

    def column_gather_sent():
        loop(Z - 1, lambda k: z_whole(far_first(k), z).wait_send())

        def chunk(zc):
            for j in range(1, X):
                x_whole(j, zc, 0).wait_send()

        loop(Z, chunk)

    def c_gram(h, k):
        return remote(gsrc, gyc.at[h, k], gyc_s.at[h, k], gyc_r.at[h, k], at_c(k))

    def c_scatter(h, k):
        return remote(scat.at[h, (c + k) % C], ypc.at[h], sc_s.at[h, k], sc_r.at[h], at_c(k))

    def row_product(h, factor):
        def receive(k, gram):
            zc = (z + Z - near_first(k)) % Z
            for j in range(1, X):
                x_whole(j, zc, -j).wait_recv()
            block = gath[zc]
            if factor is not None:
                block = dot(factor, block, HIGH)
            ybuf[zc] = block
            high, low = split(block)
            ysplit[zc] = jnp.concatenate([high, low], axis=0)
            return gram + gram_planes(block[:K], block[K:])

        gsrc[...] = lax.fori_loop(0, Z, receive, jnp.zeros((K, 128), F32))
        for k in range(1, C):
            c_gram(h, k).start()

        @pl.when(c == z)
        def _():
            for t in range(4):
                chunk = ybuf.at[2 * x + t // 2]
                part_lanes = slice((t % 2) * 128, (t % 2) * 128 + 128)
                even, odd = pack_pair(chunk[:K, part_lanes], chunk[K:, part_lanes])
                scat[h, 2 * t], scat[h, 2 * t + 1] = even, odd
            for k in range(1, C):
                c_scatter(h, k).start()
            ypc[h] = scat[h, c]

        acc[...] = jnp.zeros_like(acc)
        acc2[...] = jnp.zeros_like(acc2)

        def chunk(k):
            acc[...] += dot_nt(ysplit[k], hhi[k])
            acc2[...] += dot_nt(ysplit[k, : 2 * K], hlo[k])

        loop(Z, chunk)
        total = acc[: 2 * K] + acc[2 * K :] + acc2[...]
        re = total[:K, :512] - total[K:, 512:]
        im = total[K:, :512] + total[:K, 512:]
        for t in range(4):
            even, odd = pack_pair(re[:, 128 * t : 128 * t + 128], im[:, 128 * t : 128 * t + 128])
            pk[2 * t], pk[2 * t + 1] = even, odd

    def c_part(k):
        return remote(pk.at[(c + k) % C], rsy.at[k], rsy_s.at[k], rsy_r.at[k], at_c(k))

    def row_sum_start():
        for k in range(1, C):
            c_part(k).start()

    def row_sum():
        total = pk[c]
        for k in range(1, C):
            c_part(k).wait_recv()
            total = total + rsy[k]
        return total

    def c_factor(h):
        total = gsrc[...]
        for k in range(1, C):
            c_gram(h, k).wait_recv()
            total = total + gyc[h, k]
        return inverse_factor(total * (1.0 / N))

    def scattered(h):
        @pl.when(c != z)
        def _():
            c_scatter(h, 1).wait_recv()

        return ypc[h]

    def row_product_sent(h):
        for k in range(1, C):
            c_part(k).wait_send()
            c_gram(h, k).wait_send()

        @pl.when(c == z)
        def _():
            for k in range(1, C):
                c_scatter(h, k).wait_send()

    column_product(True)
    column_gather(column_sum())
    row_product(0, None)
    row_sum_start()
    z2_piece = row_sum()
    gy[c] = z2_piece

    def c_whole(k, src):
        return remote(gy.at[src], gy.at[src], agy_s.at[k], agy_r.at[k], at_c(k))

    for k in range(1, C):
        c_whole(k, c).start()
    inv1 = c_factor(0)
    y1_piece = scattered(0)
    y2_piece = apply_packed(inv1, z2_piece)
    fsrc[K : 2 * K] = gram_packed(v_piece, y1_piece)
    fsrc[2 * K : 3 * K] = conj_apply_packed(inv1, gram_packed(y1_piece, y2_piece))
    for k in range(1, C):
        c_whole(k, (c + C - k) % C).wait_recv()
    re, im = [], []
    for t in range(4):
        pair_re, pair_im = unpack_pair(gy[2 * t], gy[2 * t + 1])
        re.append(pair_re)
        im.append(pair_im)
    block = jnp.concatenate([jnp.concatenate(re, axis=1), jnp.concatenate(im, axis=1)], axis=0)
    block = dot(embedded(inv1), block, HIGH)
    y2_re, y2_im = block[:K], block[K:]
    set_left(y2_re, y2_im)
    gxs[...] = gram_planes(y2_re, y2_im)

    def x_gram(j):
        return remote(gxs, gx.at[j], gx_s.at[j], gx_r.at[j], at_x(j))

    def z_gram(o):
        return remote(gzs, gz.at[o], gz_s.at[o], gz_r.at[o], at_z(o))

    for j in range(1, X):
        x_gram(j).start()
    column_sum_sent()
    column_gather_sent()
    row_product_sent(0)
    column_product(False)
    total = gxs[...]
    for j in range(1, X):
        x_gram(j).wait_recv()
        total = total + gx[j]
    gzs[...] = total
    for o in range(1, Z):
        z_gram(o).start()
    column_gather(column_sum())
    total = gzs[...]
    for o in range(1, Z):
        z_gram(o).wait_recv()
        total = total + gz[o]
    inv2 = inverse_factor(total * (1.0 / N))
    row_product(1, embedded(inv2))
    row_sum_start()
    inv3 = c_factor(1)
    y3_piece = scattered(1)
    fsrc[3 * K : 4 * K] = conj_apply_packed(inv2, gram_packed(y2_piece, y3_piece))
    y4_piece = apply_packed(inv3, row_sum())
    fsrc[:K] = gram_packed(y4_piece, y4_piece)
    fsrc[4 * K : 5 * K] = conj_apply_packed(inv3, gram_packed(y3_piece, y4_piece))
    fsrc[5 * K :] = jnp.zeros((256 - 5 * K, 128), F32)


    def slab(k):
        return pl.ds(pl.multiple_of(((c + k) % C) * 32, 32), 32)

    def f_c(k):
        return remote(fsrc.at[slab(k)], fy.at[k], fy_s.at[k], fy_r.at[k], at_c(k))

    def f_x(j):
        return remote(fxs, fx.at[j], fx_s.at[j], fx_r.at[j], at_x(j))

    def f_z(o):
        return remote(fzs, fz.at[o], fz_s.at[o], fz_r.at[o], at_z(o))

    def f_all(k, shift):
        return remote(fall.at[slab(shift)], fall.at[slab(shift)], fa_s.at[k], fa_r.at[k], at_c(k))

    for k in range(1, C):
        f_c(k).start()
    total = fsrc[slab(0)]
    for k in range(1, C):
        f_c(k).wait_recv()
        total = total + fy[k]
    fxs[...] = total
    for j in range(1, X):
        f_x(j).start()
    for j in range(1, X):
        f_x(j).wait_recv()
        total = total + fx[j]
    fzs[...] = total
    for o in range(1, Z):
        f_z(o).start()
    for o in range(1, Z):
        f_z(o).wait_recv()
        total = total + fz[o]
    fall[slab(0)] = total * (1.0 / N)
    for k in range(1, C):
        f_all(k, 0).start()
    for k in range(1, C):
        f_all(k, C - k).wait_recv()
    value = apply_packed(inverse_factor(fall[:K]), y4_piece)
    basis[0] = value[:, :64]
    basis[1] = pltpu.roll(value, 64, 1)[:, :64]
    for t in range(ITERS):
        value = fall[K * (t + 1) : K * (t + 2)]
        ritz[t, 0] = value[:, :K]
        ritz[t, 1] = pltpu.roll(value, 64, 1)[:, :K]

    column_sum_sent()
    column_gather_sent()
    row_product_sent(1)
    for k in range(1, C):
        c_whole(k, c).wait_send()
        f_c(k).wait_send()
        f_all(k, 0).wait_send()
    for j in range(1, X):
        x_gram(j).wait_send()
        f_x(j).wait_send()
    for o in range(1, Z):
        z_gram(o).wait_send()
        f_z(o).wait_send()


def solution(mesh):
    dma = pltpu.SemaphoreType.DMA
    packed = (K, 128)
    scratch = [
        pltpu.VMEM((Z, 2, 512, CH), F32),
        pltpu.VMEM((Z, 1024, CH), BF16),
        pltpu.VMEM((Z, 1024, CH), BF16),
        pltpu.VMEM((4 * K, 1024), BF16),
        pltpu.VMEM((Z, 2 * K, CH), F32),
        pltpu.VMEM((X - 1, Z, RB, CH), F32),
        pltpu.VMEM((Z, RB, CH), F32),
        pltpu.VMEM((Z, RB, CH), F32),
        pltpu.VMEM((Z, 2 * K, CH), F32),
        pltpu.VMEM((Z, 2 * K, CH), F32),
        pltpu.VMEM((Z, 4 * K, CH), BF16),
        pltpu.VMEM((4 * K, 1024), F32),
        pltpu.VMEM((2 * K, 1024), F32),
        pltpu.VMEM((C, *packed), F32),
        pltpu.VMEM((C, *packed), F32),
        pltpu.VMEM((C, *packed), F32),
        pltpu.VMEM((2, C, *packed), F32),
        pltpu.VMEM((2, *packed), F32),
        pltpu.VMEM(packed, F32),
        pltpu.VMEM((2, C, *packed), F32),
        pltpu.VMEM(packed, F32),
        pltpu.VMEM((X, *packed), F32),
        pltpu.VMEM(packed, F32),
        pltpu.VMEM((Z, *packed), F32),
        pltpu.VMEM((256, 128), F32),
        pltpu.VMEM((C, 32, 128), F32),
        pltpu.VMEM((32, 128), F32),
        pltpu.VMEM((X, 32, 128), F32),
        pltpu.VMEM((32, 128), F32),
        pltpu.VMEM((Z, 32, 128), F32),
        pltpu.VMEM((256, 128), F32),
        dma((Z,)),
        dma((X - 1, Z)), dma((X - 1, Z)), dma((Z,)), dma((Z,)),
        dma((Z,)), dma((Z,)), dma((X - 1, Z)), dma((X - 1, Z)),
        dma((C,)), dma((C,)), dma((C,)), dma((C,)),
        dma((2, C)), dma((2,)), dma((2, C)), dma((2, C)),
        dma((X,)), dma((X,)), dma((Z,)), dma((Z,)),
        dma((C,)), dma((C,)), dma((X,)), dma((X,)), dma((Z,)), dma((Z,)), dma((C,)), dma((C,)),
    ]
    vmem = pl.BlockSpec(memory_space=pltpu.VMEM)

    def body(coupling, initial):
        return pl.pallas_call(
            kernel,
            name="subspace",
            out_shape=(
                jax.ShapeDtypeStruct((2, K, 64), F32),
                jax.ShapeDtypeStruct((ITERS, 2, K, K), F32),
            ),
            in_specs=[pl.BlockSpec(memory_space=pl.ANY), vmem],
            out_specs=(vmem, vmem),
            scratch_shapes=scratch,
            compiler_params=pltpu.CompilerParams(
                collective_id=0, has_side_effects=True, vmem_limit_bytes=56 * 1024 * 1024
            ),
        )(coupling, initial)

    return jax.shard_map(
        body,
        mesh=mesh,
        in_specs=(P(None, "rows", "cols"), P(None, None, "rows")),
        out_specs=(P(None, None, ("rows", "cols")), P()),
        check_vma=False,
    )
```

```python
import jax
import jax.numpy as jnp
from jax import lax
from jax.experimental import pallas as pl
from jax.experimental.pallas import tpu as pltpu
from jax.sharding import PartitionSpec as P

N = 16384
K = 48
ITERS = 4
X, Z, C = 4, 8, 8
CH = 256
HALF = K // 2
F32, BF16 = jnp.float32, jnp.bfloat16
MESH = pl.DeviceIdType.MESH
HIGH = lax.Precision.HIGHEST
NT = (((1,), (1,)), ((), ()))


def dot(a, b, precision=None):
    return jnp.dot(a, b, precision=precision, preferred_element_type=F32)


def dot_nt(a, b, precision=None):
    return lax.dot_general(a, b, NT, precision=precision, preferred_element_type=F32)


def split(value):
    high = value.astype(BF16)
    return high, (value - high.astype(F32)).astype(BF16)


def lanes(shape):
    return lax.broadcasted_iota(jnp.int32, shape, 1)


def turned(packed):
    rolled = pltpu.roll(packed, 64, 1)
    return jnp.where(lanes(packed.shape) < 64, rolled, -rolled)


def stacked_rows(first, second):
    gap = jnp.zeros((64 - K, first.shape[1]), first.dtype)
    return jnp.concatenate([first, gap, second, gap], axis=0)


def gram_packed(left, right):
    return dot_nt(left, stacked_rows(right, turned(right)), HIGH)


def gram_planes(re, im):
    return dot_nt(re, stacked_rows(re, im), HIGH) + dot_nt(im, stacked_rows(im, -re), HIGH)


def planes_of(packed):
    low = lanes(packed.shape) < 64
    return jnp.where(low, packed, 0.0), jnp.where(low, pltpu.roll(packed, 64, 1), 0.0)


def apply_packed(matrix, packed):
    re, im = planes_of(matrix)
    return dot(re[:, :K], packed, HIGH) - dot(im[:, :K], turned(packed), HIGH)


def conj_apply_packed(matrix, packed):
    re, im = planes_of(matrix)
    return dot(re[:, :K], packed, HIGH) + dot(im[:, :K], turned(packed), HIGH)


def embedded(matrix, h):
    re, im = planes_of(matrix)
    rows, width = slice(HALF * h, HALF * h + HALF), HALF * (h + 1)
    upper = re[rows] - pltpu.roll(im[rows], width, 1)
    lower = im[rows] + pltpu.roll(re[rows], width, 1)
    return jnp.concatenate([upper, lower], axis=0)[:, : 2 * width]


def inverse_factor(gram):
    lane = lanes((K, 128))
    row = lax.broadcasted_iota(jnp.int32, (K, 128), 0)
    low = lane < 64
    re = jnp.where(low, gram, jnp.where(lane - 64 == row, 1.0, 0.0))
    im = jnp.where(low, pltpu.roll(gram, 64, 1), 0.0)
    done_re, done_im = [], []
    for base in range(0, K, 8):
        below = lax.broadcasted_iota(jnp.int32, (K - base, 1), 0)
        for s in range(8):
            j = base + s
            row_re, row_im = re[s : s + 1], im[s : s + 1]
            inv = 1.0 / re[s : s + 1, j : j + 1]
            m_re = jnp.where(below > s, re[:, j : j + 1] * inv, 0.0)
            m_im = jnp.where(below > s, im[:, j : j + 1] * inv, 0.0)
            re, im = (
                re - (m_re * row_re - m_im * row_im),
                im - (m_re * row_im + m_im * row_re),
            )
        done_re.append(re[:8])
        done_im.append(im[:8])
        re, im = re[8:], im[8:]
    re = jnp.concatenate(done_re, axis=0)
    im = jnp.concatenate(done_im, axis=0)
    pivot = jnp.sum(jnp.where(lane == row, re, 0.0), axis=1, keepdims=True)
    scale = 1.0 / jnp.sqrt(pivot)
    return jnp.where(low, pltpu.roll(re, 64, 1), im) * scale


def pack_pair(re, im):
    low = lanes(re.shape) < 64
    even = jnp.where(low, re, pltpu.roll(im, 64, 1))
    odd = jnp.where(low, pltpu.roll(re, 64, 1), im)
    return even, odd


def unpack_pair(even, odd):
    low = lanes(even.shape) < 64
    re = jnp.where(low, even, pltpu.roll(odd, 64, 1))
    im = jnp.where(low, pltpu.roll(even, 64, 1), odd)
    return re, im


def far_first(k):
    return 4 + (k // 2) * (1 - k % 2) - ((k + 1) // 2) * (k % 2)


def near_first(k):
    return (8 + far_first(7 - k)) % 8


def kernel(coupling, initial, basis, ritz, *scratch):
    (
        stage, hhi, hlo, lhs, part, rsx, red, rsz, gath, ybuf, ysplit, acc, acc2,
        pk, rsy, gy, vpk, scat, ypc, gsrc, gyc, gxs, gx, gzs, gz,
        g4, g4y, g4x, g4z, psrc, py, px, pz, pall,
        hsem, rsx_s, rsx_r, rsz_s, rsz_r, agz_s, agz_r, agx_s, agx_r,
        rsy_s, rsy_r, agy_s, agy_r, sc_s, sc_r, gyc_s, gyc_r, gx_s, gx_r, gz_s, gz_r,
        g4y_s, g4y_r, g4x_s, g4x_r, g4z_s, g4z_r, py_s, py_r, px_s, px_r, pz_s, pz_r, pa_s, pa_r,
    ) = scratch
    r, c = lax.axis_index("rows"), lax.axis_index("cols")
    z, x = r // X, r % X

    def at_x(j):
        return (z * X + (x + j) % X, c)

    def at_z(o):
        return (((z + o) % Z) * X + x, c)

    def at_c(k):
        return (r, (c + k) % C)

    def remote(src, dst, send, recv, dev):
        return pltpu.make_async_remote_copy(
            src_ref=src, dst_ref=dst, send_sem=send, recv_sem=recv,
            device_id=dev, device_id_type=MESH,
        )

    def loop(n, f):
        def step(i, carry):
            f(i)
            return carry

        lax.fori_loop(0, n, step, 0)

    def load(k):
        zc = (z + far_first(k)) % Z
        columns = pl.ds(pl.multiple_of(zc * CH, CH), CH)
        return pltpu.make_async_copy(coupling.at[:, :, columns], stage.at[zc], hsem.at[zc])

    loop(Z, lambda k: load(k).start())

    barrier = pltpu.get_barrier_semaphore()
    partners = [at_x(j) for j in range(1, X)] + [at_z(o) for o in range(1, Z)]
    partners += [at_c(k) for k in range(1, C)]
    for dev in partners:
        pl.semaphore_signal(barrier, inc=1, device_id=dev, device_id_type=MESH)

    def set_left(h, re, im):
        top = jnp.concatenate([re, im], axis=1)
        bottom = jnp.concatenate([im, -re], axis=1)
        high, low = split(jnp.concatenate([top, bottom], axis=0))
        lhs[h] = jnp.concatenate([high, low], axis=0)


    def x_part(h, j, zc):
        return remote(
            part.at[h, zc, (x + j) % X], rsx.at[h, j - 1, zc],
            rsx_s.at[h, j - 1, zc], rsx_r.at[h, j - 1, zc], at_x(j),
        )

    def z_part(h, o, zc):
        return remote(red.at[h, zc], rsz.at[h, o], rsz_s.at[h, o], rsz_r.at[h, o], at_z(o))

    def send_parts(h, zc):
        for j in (2, 1, 3):
            x_part(h, j, zc).start()

    def column_product(h, load_first, send):
        def chunk(k):
            zc = (z + far_first(k)) % Z
            if load_first:
                load(k).wait()
                for t in range(0, 1024, 128):
                    high, low = split(stage[zc, t // 512, t % 512 : t % 512 + 128])
                    hhi[zc, t : t + 128] = high
                    hlo[zc, t : t + 128] = low
            both = dot(lhs[h], hhi[zc])
            total = both[:K] + both[K:] + dot(lhs[h, :K], hlo[zc])
            for q in range(X):
                part[h, zc, q] = total[
                    HALF * (q // 2) : HALF * (q // 2) + HALF, 128 * (q % 2) : 128 * (q % 2) + 128
                ]
            if send:
                send_parts(h, zc)

        loop(Z, chunk)

    def column_sum(h):
        def chunk(k):
            o = far_first(k)
            zc = (z + o) % Z
            total = part[h, zc, x]
            for j in range(1, X):
                x_part(h, j, zc).wait_recv()
                total = total + rsx[h, j - 1, zc]
            red[h, zc] = total

            @pl.when(k < Z - 1)
            def _():
                z_part(h, o, zc).start()

        loop(Z, chunk)

    def sums_sent(h):
        def chunk(k):
            o = far_first(k)
            zc = (z + o) % Z
            for j in range(1, X):
                x_part(h, j, zc).wait_send()
                x_whole(h, j, zc, 0).wait_send()

            @pl.when(k < Z - 1)
            def _():
                z_part(h, o, zc).wait_send()
                z_whole(h, o, z).wait_send()

        loop(Z, chunk)


    def z_whole(h, o, zc):
        piece = gath.at[h, zc, x]
        return remote(piece, piece, agz_s.at[h, o], agz_r.at[h, o], at_z(o))

    def x_whole(h, j, zc, shift):
        piece = gath.at[h, zc, (x + shift) % X]
        return remote(piece, piece, agx_s.at[h, j - 1, zc], agx_r.at[h, j - 1, zc], at_x(j))

    def column_gather(h):
        total = red[h, z]
        for o in range(1, Z):
            z_part(h, o, z).wait_recv()
            total = total + rsz[h, o]
        gath[h, z, x] = total
        loop(Z - 1, lambda k: z_whole(h, far_first(k), z).start())
        for j in range(1, X):
            x_whole(h, j, z, 0).start()

    def column_forward(h):
        def forward(k):
            o = near_first(k + 1)
            zc = (z + Z - o) % Z
            z_whole(h, o, zc).wait_recv()
            for j in (2, 1, 3):
                x_whole(h, j, zc, 0).start()

        loop(Z - 1, forward)

    def column_exchange():
        for h in range(2):
            column_sum(h)
        for h in range(2):
            column_gather(h)
        for h in range(2):
            column_forward(h)

    def c_gram(t, k):
        return remote(gsrc, gyc.at[t, k], gyc_s.at[t, k], gyc_r.at[t, k], at_c(k))

    def c_scatter(t, k):
        return remote(scat.at[t, (c + k) % C], ypc.at[t], sc_s.at[t, k], sc_r.at[t], at_c(k))

    def c_part(h, k):
        return remote(pk.at[h, (c + k) % C], rsy.at[h, k], rsy_s.at[h, k], rsy_r.at[h, k], at_c(k))

    def gathered(h, zc):
        left = jnp.concatenate([gath[h, zc, 0], gath[h, zc, 2]], axis=0)
        right = jnp.concatenate([gath[h, zc, 1], gath[h, zc, 3]], axis=0)
        return jnp.concatenate([left, right], axis=1)

    def row_receive(h, inverse):
        if inverse is not None:
            factor = embedded(inverse, h)

        def receive(k):
            zc = (z + Z - near_first(k)) % Z
            for j in range(1, X):
                x_whole(h, j, zc, X - j).wait_recv()
            block = gathered(h, zc)
            if inverse is not None:
                if h == 1:
                    other = gathered(0, zc)
                    block = jnp.concatenate([other[:HALF], block[:HALF], other[HALF:], block[HALF:]], axis=0)
                block = dot(factor, block, HIGH)
            ybuf[0, zc, HALF * h : HALF * h + HALF] = block[:HALF]
            ybuf[1, zc, HALF * h : HALF * h + HALF] = block[HALF:]
            high, low = split(block)
            ysplit[h, zc] = jnp.concatenate([high, low], axis=0)

        loop(Z, receive)

    def row_gram(t):
        gsrc[...] = lax.fori_loop(
            0, Z, lambda k, gram: gram + gram_planes(ybuf[0, k], ybuf[1, k]), jnp.zeros((K, 128), F32)
        )
        for k in range(1, C):
            c_gram(t, k).start()

        @pl.when(c == z)
        def _():
            for q in range(4):
                part_lanes = slice((q % 2) * 128, (q % 2) * 128 + 128)
                even, odd = pack_pair(
                    ybuf[0, 2 * x + q // 2, :, part_lanes], ybuf[1, 2 * x + q // 2, :, part_lanes]
                )
                scat[t, 2 * q], scat[t, 2 * q + 1] = even, odd
            for k in range(1, C):
                c_scatter(t, k).start()
            ypc[t] = scat[t, c]

    def row_product(h):
        acc[...] = jnp.zeros_like(acc)
        acc2[...] = jnp.zeros_like(acc2)

        def chunk(k):
            acc[...] += dot_nt(ysplit[h, k], hhi[k])
            acc2[...] += dot_nt(ysplit[h, k, :K], hlo[k])

        loop(Z, chunk)
        total = acc[:K] + acc[K:] + acc2[...]
        re = total[:HALF, :512] - total[HALF:, 512:]
        im = total[HALF:, :512] + total[:HALF, 512:]
        for q in range(4):
            even, odd = pack_pair(re[:, 128 * q : 128 * q + 128], im[:, 128 * q : 128 * q + 128])
            pk[h, 2 * q], pk[h, 2 * q + 1] = even, odd
        for k in range(1, C):
            c_part(h, k).start()

    def row_products(t, inverse):
        row_receive(0, inverse)
        row_product(0)
        row_receive(1, inverse)
        row_gram(t)
        row_product(1)

    def row_sum(h):
        total = pk[h, c]
        for k in range(1, C):
            c_part(h, k).wait_recv()
            total = total + rsy[h, k]
        return total

    def c_factor(t):
        total = gsrc[...]
        for k in range(1, C):
            c_gram(t, k).wait_recv()
            total = total + gyc[t, k]
        return inverse_factor(total * (1.0 / N))

    def scattered(t):
        @pl.when(c != z)
        def _():
            c_scatter(t, 1).wait_recv()

        return ypc[t]

    def row_sent(t):
        for k in range(1, C):
            for h in range(2):
                c_part(h, k).wait_send()
            c_gram(t, k).wait_send()

        @pl.when(c == z)
        def _():
            for k in range(1, C):
                c_scatter(t, k).wait_send()

    v_re, v_im = initial[0], initial[1]
    for h in range(2):
        set_left(h, v_re[HALF * h : HALF * h + HALF], v_im[HALF * h : HALF * h + HALF])
    column_product(0, True, False)
    pl.semaphore_wait(barrier, len(partners))
    loop(Z, lambda k: send_parts(0, (z + far_first(k)) % Z))
    column_product(1, False, True)
    for q in range(4):
        even, odd = pack_pair(v_re[:, 128 * q : 128 * q + 128], v_im[:, 128 * q : 128 * q + 128])
        vpk[2 * q], vpk[2 * q + 1] = even, odd
    v_piece = vpk[c]
    column_exchange()
    row_products(0, None)

    def c_whole(h, k, src):
        return remote(gy.at[h, src], gy.at[h, src], agy_s.at[h, k], agy_r.at[h, k], at_c(k))

    z2_piece = []
    for h in range(2):
        z2_piece.append(row_sum(h))
        gy[h, c] = z2_piece[h]
        for k in range(1, C):
            c_whole(h, k, c).start()
    z2_piece = jnp.concatenate(z2_piece, axis=0)
    inv1 = c_factor(0)
    for h in range(2):
        sums_sent(h)
    got_re, got_im, y2_re, y2_im = [], [], [], []
    for h in range(2):
        for k in range(1, C):
            c_whole(h, k, (c + C - k) % C).wait_recv()
        pairs = [unpack_pair(gy[h, 2 * q], gy[h, 2 * q + 1]) for q in range(4)]
        got_re.append(jnp.concatenate([pair[0] for pair in pairs], axis=1))
        got_im.append(jnp.concatenate([pair[1] for pair in pairs], axis=1))
        block = dot(embedded(inv1, h), jnp.concatenate(got_re + got_im, axis=0), HIGH)
        y2_re.append(block[:HALF])
        y2_im.append(block[HALF:])
        set_left(h, block[:HALF], block[HALF:])
        column_product(h, False, True)
    gxs[...] = gram_planes(jnp.concatenate(y2_re, axis=0), jnp.concatenate(y2_im, axis=0))

    def x_gram(j):
        return remote(gxs, gx.at[j], gx_s.at[j], gx_r.at[j], at_x(j))

    def z_gram(o):
        return remote(gzs, gz.at[o], gz_s.at[o], gz_r.at[o], at_z(o))

    for j in range(1, X):
        x_gram(j).start()
    row_sent(0)
    y2_piece = apply_packed(inv1, z2_piece)
    y1_piece = scattered(0)
    psrc[:K] = gram_packed(v_piece, y1_piece)
    psrc[K : 2 * K] = conj_apply_packed(inv1, gram_packed(y1_piece, y2_piece))
    for h in range(2):
        column_sum(h)
    total = gxs[...]
    for j in range(1, X):
        x_gram(j).wait_recv()
        total = total + gx[j]
    gzs[...] = total
    for o in range(1, Z):
        z_gram(o).start()
    for h in range(2):
        column_gather(h)
    for h in range(2):
        column_forward(h)
    total = gzs[...]
    for o in range(1, Z):
        z_gram(o).wait_recv()
        total = total + gz[o]
    inv2 = inverse_factor(total * (1.0 / N))
    row_products(1, inv2)
    inv3 = c_factor(1)
    y4_piece = apply_packed(inv3, jnp.concatenate([row_sum(0), row_sum(1)], axis=0))


    def g_c(k):
        return remote(g4.at[0], g4y.at[k], g4y_s.at[k], g4y_r.at[k], at_c(k))

    def g_x(j):
        return remote(g4.at[1], g4x.at[j], g4x_s.at[j], g4x_r.at[j], at_x(j))

    def g_z(o):
        return remote(g4.at[2], g4z.at[o], g4z_s.at[o], g4z_r.at[o], at_z(o))

    def slab(shift):
        return pl.ds(pl.multiple_of(((c + shift) % C) * HALF, 8), HALF)

    def p_c(k):
        return remote(psrc.at[slab(k)], py.at[k], py_s.at[k], py_r.at[k], at_c(k))

    def p_x(j):
        return remote(px.at[0], px.at[j], px_s.at[j], px_r.at[j], at_x(j))

    def p_z(o):
        return remote(pz.at[0], pz.at[o], pz_s.at[o], pz_r.at[o], at_z(o))

    def p_all(k, shift):
        return remote(pall.at[slab(shift)], pall.at[slab(shift)], pa_s.at[k], pa_r.at[k], at_c(k))

    def added(total, n, copy, slots):
        for i in range(1, n):
            copy(i).wait_recv()
            total = total + slots[i]
        return total

    gram = gram_packed(y4_piece, y4_piece)
    g4[0] = gram
    for k in range(1, C):
        g_c(k).start()
    y3_piece = scattered(1)
    psrc[2 * K : 3 * K] = conj_apply_packed(inv2, gram_packed(y2_piece, y3_piece))
    psrc[3 * K :] = conj_apply_packed(inv3, gram_packed(y3_piece, y4_piece))
    for k in range(1, C):
        p_c(k).start()
    gram = added(gram, C, g_c, g4y)
    g4[1] = gram
    for j in range(1, X):
        g_x(j).start()
    px[0] = added(psrc[slab(0)], C, p_c, py)
    for j in range(1, X):
        p_x(j).start()
    gram = added(gram, X, g_x, g4x)
    g4[2] = gram
    for o in range(1, Z):
        g_z(o).start()
    pz[0] = added(px[0], X, p_x, px)
    for o in range(1, Z):
        p_z(o).start()
    gram = added(gram, Z, g_z, g4z)
    pall[slab(0)] = added(pz[0], Z, p_z, pz) * (1.0 / N)
    for k in range(1, C):
        p_all(k, 0).start()
    value = apply_packed(inverse_factor(gram * (1.0 / N)), y4_piece)
    basis[0] = value[:, :64]
    basis[1] = pltpu.roll(value, 64, 1)[:, :64]
    for k in range(1, C):
        p_all(k, C - k).wait_recv()
    for t in range(ITERS):
        value = pall[K * t : K * t + K]
        ritz[t, 0] = value[:, :K]
        ritz[t, 1] = pltpu.roll(value, 64, 1)[:, :K]

    for h in range(2):
        sums_sent(h)
        for k in range(1, C):
            c_whole(h, k, c).wait_send()
    row_sent(1)
    for k in range(1, C):
        g_c(k).wait_send()
        p_c(k).wait_send()
        p_all(k, 0).wait_send()
    for j in range(1, X):
        x_gram(j).wait_send()
        g_x(j).wait_send()
        p_x(j).wait_send()
    for o in range(1, Z):
        z_gram(o).wait_send()
        g_z(o).wait_send()
        p_z(o).wait_send()


def solution(mesh):
    dma = pltpu.SemaphoreType.DMA
    packed, piece = (K, 128), (HALF, 128)
    scratch = [
        pltpu.VMEM((Z, 2, 512, CH), F32),
        pltpu.VMEM((Z, 1024, CH), BF16),
        pltpu.VMEM((Z, 1024, CH), BF16),
        pltpu.VMEM((2, 2 * K, 1024), BF16),
        pltpu.VMEM((2, Z, X, *piece), F32),
        pltpu.VMEM((2, X - 1, Z, *piece), F32),
        pltpu.VMEM((2, Z, *piece), F32),
        pltpu.VMEM((2, Z, *piece), F32),
        pltpu.VMEM((2, Z, X, *piece), F32),
        pltpu.VMEM((2, Z, K, CH), F32),
        pltpu.VMEM((2, Z, 2 * K, CH), BF16),
        pltpu.VMEM((2 * K, 1024), F32),
        pltpu.VMEM((K, 1024), F32),
        pltpu.VMEM((2, C, *piece), F32),
        pltpu.VMEM((2, C, *piece), F32),
        pltpu.VMEM((2, C, *piece), F32),
        pltpu.VMEM((C, *packed), F32),
        pltpu.VMEM((2, C, *packed), F32),
        pltpu.VMEM((2, *packed), F32),
        pltpu.VMEM(packed, F32),
        pltpu.VMEM((2, C, *packed), F32),
        pltpu.VMEM(packed, F32),
        pltpu.VMEM((X, *packed), F32),
        pltpu.VMEM(packed, F32),
        pltpu.VMEM((Z, *packed), F32),
        pltpu.VMEM((3, *packed), F32),
        pltpu.VMEM((C, *packed), F32),
        pltpu.VMEM((X, *packed), F32),
        pltpu.VMEM((Z, *packed), F32),
        pltpu.VMEM((4 * K, 128), F32),
        pltpu.VMEM((C, *piece), F32),
        pltpu.VMEM((X, *piece), F32),
        pltpu.VMEM((Z, *piece), F32),
        pltpu.VMEM((4 * K, 128), F32),
        dma((Z,)),
        dma((2, X - 1, Z)), dma((2, X - 1, Z)), dma((2, Z)), dma((2, Z)),
        dma((2, Z)), dma((2, Z)), dma((2, X - 1, Z)), dma((2, X - 1, Z)),
        dma((2, C)), dma((2, C)), dma((2, C)), dma((2, C)),
        dma((2, C)), dma((2,)), dma((2, C)), dma((2, C)),
        dma((X,)), dma((X,)), dma((Z,)), dma((Z,)),
        dma((C,)), dma((C,)), dma((X,)), dma((X,)), dma((Z,)), dma((Z,)),
        dma((C,)), dma((C,)), dma((X,)), dma((X,)), dma((Z,)), dma((Z,)), dma((C,)), dma((C,)),
    ]
    vmem = pl.BlockSpec(memory_space=pltpu.VMEM)

    def body(coupling, initial):
        return pl.pallas_call(
            kernel,
            name="subspace",
            out_shape=(
                jax.ShapeDtypeStruct((2, K, 64), F32),
                jax.ShapeDtypeStruct((ITERS, 2, K, K), F32),
            ),
            in_specs=[pl.BlockSpec(memory_space=pl.ANY), vmem],
            out_specs=(vmem, vmem),
            scratch_shapes=scratch,
            compiler_params=pltpu.CompilerParams(
                collective_id=0, has_side_effects=True, vmem_limit_bytes=56 * 1024 * 1024
            ),
        )(coupling, initial)

    return jax.shard_map(
        body,
        mesh=mesh,
        in_specs=(P(None, "rows", "cols"), P(None, None, "rows")),
        out_specs=(P(None, None, ("rows", "cols")), P()),
        check_vma=False,
    )
```

```python
import jax
import jax.numpy as jnp
from jax import lax
from jax.experimental import pallas as pl
from jax.experimental.pallas import tpu as pltpu
from jax.sharding import PartitionSpec as P

N = 16384
K = 48
ITERS = 4
X, Z, C = 4, 8, 8
CH = 256
RB = 2 * K // X
F32, BF16 = jnp.float32, jnp.bfloat16
MESH = pl.DeviceIdType.MESH
HIGH = lax.Precision.HIGHEST
NT = (((1,), (1,)), ((), ()))


def dot(a, b, precision=None):
    return jnp.dot(a, b, precision=precision, preferred_element_type=F32)


def dot_nt(a, b, precision=None):
    return lax.dot_general(a, b, NT, precision=precision, preferred_element_type=F32)


def split(value):
    high = value.astype(BF16)
    return high, (value - high.astype(F32)).astype(BF16)


def lanes(shape):
    return lax.broadcasted_iota(jnp.int32, shape, 1)


def turned(packed):
    rolled = pltpu.roll(packed, 64, 1)
    return jnp.where(lanes(packed.shape) < 64, rolled, -rolled)


def stacked_rows(first, second):
    gap = jnp.zeros((64 - K, first.shape[1]), first.dtype)
    return jnp.concatenate([first, gap, second, gap], axis=0)


def gram_packed(left, right):
    return dot_nt(left, stacked_rows(right, turned(right)), HIGH)


def gram_planes(re, im):
    return dot_nt(re, stacked_rows(re, im), HIGH) + dot_nt(im, stacked_rows(im, -re), HIGH)


def planes_of(packed):
    low = lanes(packed.shape) < 64
    return jnp.where(low, packed, 0.0), jnp.where(low, pltpu.roll(packed, 64, 1), 0.0)


def apply_packed(matrix, packed):
    re, im = planes_of(matrix)
    return dot(re[:, :K], packed, HIGH) - dot(im[:, :K], turned(packed), HIGH)


def conj_apply_packed(matrix, packed):
    re, im = planes_of(matrix)
    return dot(re[:, :K], packed, HIGH) + dot(im[:, :K], turned(packed), HIGH)


def embedded(matrix):
    re, im = planes_of(matrix)
    upper = re - pltpu.roll(im, K, 1)
    lower = im + pltpu.roll(re, K, 1)
    return jnp.concatenate([upper, lower], axis=0)[:, : 2 * K]


def factor_steps(gram, result):
    lane = lanes((K, 128))
    row = lax.broadcasted_iota(jnp.int32, (K, 128), 0)
    low = lane < 64
    re = jnp.where(low, gram, jnp.where(lane - 64 == row, 1.0, 0.0))
    im = jnp.where(low, pltpu.roll(gram, 64, 1), 0.0)
    done_re, done_im = [], []
    for base in range(0, K, 8):
        below = lax.broadcasted_iota(jnp.int32, (K - base, 1), 0)
        for s in range(8):
            j = base + s
            row_re, row_im = re[s : s + 1], im[s : s + 1]
            inv = 1.0 / re[s : s + 1, j : j + 1]
            m_re = jnp.where(below > s, re[:, j : j + 1] * inv, 0.0)
            m_im = jnp.where(below > s, im[:, j : j + 1] * inv, 0.0)
            re, im = (
                re - (m_re * row_re - m_im * row_im),
                im - (m_re * row_im + m_im * row_re),
            )
        done_re.append(re[:8])
        done_im.append(im[:8])
        re, im = re[8:], im[8:]
        yield
    re = jnp.concatenate(done_re, axis=0)
    im = jnp.concatenate(done_im, axis=0)
    pivot = jnp.sum(jnp.where(lane == row, re, 0.0), axis=1, keepdims=True)
    scale = 1.0 / jnp.sqrt(pivot)
    result.append(jnp.where(low, pltpu.roll(re, 64, 1), im) * scale)


def inverse_factor(gram):
    result = []
    for _ in factor_steps(gram, result):
        pass
    return result[0]


def both_sides(matrix, packed):
    left = conj_apply_packed(matrix, packed)
    low = lanes(matrix.shape) < 64
    return dot_nt(left, stacked_rows(jnp.where(low, matrix, -matrix), pltpu.roll(matrix, 64, 1)), HIGH)


def pack_pair(re, im):
    low = lanes(re.shape) < 64
    even = jnp.where(low, re, pltpu.roll(im, 64, 1))
    odd = jnp.where(low, pltpu.roll(re, 64, 1), im)
    return even, odd


def unpack_pair(even, odd):
    low = lanes(even.shape) < 64
    re = jnp.where(low, even, pltpu.roll(odd, 64, 1))
    im = jnp.where(low, pltpu.roll(even, 64, 1), odd)
    return re, im


def far_first(k):
    return 4 + (k >> 1) * (1 - (k & 1)) - ((k + 1) >> 1) * (k & 1)


def near_first(k):
    return far_first(7 - k) & 7


def kernel(coupling, initial, basis, ritz, *scratch):
    (
        stage, hhi, hlo, lhs, part, rsx, mixed, red, rsz, gath, ybuf, acc, acc2,
        pk, rsy, gy, scat, ypc, gsrc, gyc, gxs, gx, gzs, gz,
        g4, g4y, g4x, g4z, psrc, py, px, pz, pall,
        hsem, rsx_s, rsx_r, rsz_s, rsz_r, agz_s, agz_r, agx_s, agx_r,
        rsy_s, rsy_r, agy_s, agy_r, sc_s, sc_r, gyc_s, gyc_r, gx_s, gx_r, gz_s, gz_r,
        g4y_s, g4y_r, g4x_s, g4x_r, g4z_s, g4z_r, py_s, py_r, px_s, px_r, pz_s, pz_r, pa_s, pa_r,
    ) = scratch
    r, c = lax.axis_index("rows"), lax.axis_index("cols")
    z, x = r >> 2, r & 3

    def at_x(j):
        return (z * X + ((x + j) & 3), c)

    def at_z(o):
        return (((z + o) & 7) * X + x, c)

    def at_c(k):
        return (r, (c + k) & 7)

    def remote(src, dst, send, recv, dev):
        return pltpu.make_async_remote_copy(
            src_ref=src, dst_ref=dst, send_sem=send, recv_sem=recv,
            device_id=dev, device_id_type=MESH,
        )

    def loop(n, f):
        def step(i, carry):
            f(i)
            return carry

        lax.fori_loop(0, n, step, 0)

    def rows_of(j):
        return pl.ds(pl.multiple_of(((x + j) & 3) * RB, 8), RB)

    def far(k):
        return (z + far_first(k)) & 7

    def near(k):
        return (z + 8 - near_first(k)) & 7

    def side(k):
        return 1 - 2 * (k & 1)

    def load(k):
        columns = pl.ds(pl.multiple_of(far(k) * CH, CH), CH)
        return pltpu.make_async_copy(coupling.at[:, :, columns], stage.at[far(k)], hsem.at[far(k)])

    loop(Z, lambda k: load(k).start())

    barrier = pltpu.get_barrier_semaphore()
    partners = [at_x(j) for j in range(1, X)] + [at_z(o) for o in range(1, Z)]
    partners += [at_c(k) for k in range(1, C)]
    for dev in partners:
        pl.semaphore_signal(barrier, inc=1, device_id=dev, device_id_type=MESH)

    def set_left(re, im):
        top = jnp.concatenate([re, im], axis=1)
        bottom = jnp.concatenate([im, -re], axis=1)
        high, low = split(jnp.concatenate([top, bottom], axis=0))
        lhs[...] = jnp.concatenate([high, low], axis=0)


    def x_part(k, which):
        zc, s = far(k), side(k)
        source = [part.at[zc, rows_of(2)], part.at[zc, rows_of(-s)], mixed.at[zc]][which]
        return remote(
            source, rsx.at[which, zc], rsx_s.at[which, zc], rsx_r.at[which, zc], at_x([s, -s, s][which])
        )

    def z_part(k):
        o = far_first(k)
        return remote(red.at[far(k)], rsz.at[o], rsz_s.at[o], rsz_r.at[o], at_z(o))

    def send_parts(k):
        x_part(k, 0).start()
        x_part(k, 1).start()

    def column_product(load_first, send):
        def chunk(k):
            zc = far(k)
            if load_first:
                load(k).wait()
                for t in range(0, 1024, 128):
                    high, low = split(stage[zc, t // 512, t % 512 : t % 512 + 128])
                    hhi[zc, t : t + 128] = high
                    hlo[zc, t : t + 128] = low
            both = dot(lhs[...], hhi[zc])
            part[zc] = both[: 2 * K] + both[2 * K :] + dot(lhs[: 2 * K], hlo[zc])
            if send:
                send_parts(k)

        loop(Z, chunk)

    def column_mix():
        def chunk(k):
            x_part(k, 0).wait_recv()
            mixed[far(k)] = part[far(k), rows_of(side(k))] + rsx[0, far(k)]
            x_part(k, 2).start()

        loop(Z, chunk)

    def column_sum():
        def chunk(k):
            zc = far(k)
            x_part(k, 1).wait_recv()
            x_part(k, 2).wait_recv()
            red[zc] = part[zc, rows_of(0)] + rsx[1, zc] + rsx[2, zc]

            @pl.when(k < Z - 1)
            def _():
                z_part(k).start()

        loop(Z, chunk)


    def z_whole(o, zc):
        block = gath.at[zc, rows_of(0)]
        return remote(block, block, agz_s.at[o], agz_r.at[o], at_z(o))

    def x_whole(k, which, sent=True):
        zc, s = near(k), side(k)
        straight = k >= Z - 2
        shift = 0 if sent and (which < 2 or straight) else (-s if sent else [-s, s, 2][which])
        block = gath.at[zc, rows_of(shift)]
        dev = at_x([s, -s, 2 if straight else s][which])
        return remote(block, block, agx_s.at[which, k], agx_r.at[which, k], dev)

    def column_gather(steps):
        total = red[z]
        for k in range(Z - 1):
            z_part(k).wait_recv()
            total = total + rsz[far_first(k)]
        gath[z, rows_of(0)] = total
        for k in range(Z - 1):
            z_whole(far_first(k), z).start()

        def pass_on(k):
            x_whole(k, 0, False).wait_recv()
            x_whole(k, 2).start()

        for k in range(Z):
            if k > 0:
                z_whole(near_first(k), near(k)).wait_recv()
            x_whole(k, 0).start()
            x_whole(k, 1).start()
            if k >= Z - 2:
                x_whole(k, 2).start()
            if k >= 2:
                pass_on(k - 2)
            next(steps, None)
        for _ in steps:
            pass

    def column_sent():
        for k in range(Z):
            for which in range(3):
                x_part(k, which).wait_send()
                x_whole(k, which).wait_send()
            if k < Z - 1:
                z_part(k).wait_send()
                z_whole(far_first(k), z).wait_send()

    def c_gram(t, k):
        return remote(gsrc, gyc.at[t, k], gyc_s.at[t, k], gyc_r.at[t, k], at_c(k))

    def c_scatter(t, k):
        return remote(scat.at[t, (c + k) & 7], ypc.at[t], sc_s.at[t, k], sc_r.at[t], at_c(k))

    def c_part(k):
        return remote(pk.at[(c + k) & 7], rsy.at[k], rsy_s.at[k], rsy_r.at[k], at_c(k))

    def row_product(t, factor):
        acc[...] = jnp.zeros_like(acc)
        acc2[...] = jnp.zeros_like(acc2)
        gsrc[...] = jnp.zeros_like(gsrc)
        for k in range(Z):
            zc = near(k)
            if k < Z - 2:
                x_whole(k, 1, False).wait_recv()
                x_whole(k, 2, False).wait_recv()
            else:
                for which in range(3):
                    x_whole(k, which, False).wait_recv()
            block = gath[zc]
            if factor is not None:
                block = dot(factor, block, HIGH)
            ybuf[zc] = block
            high, low = split(block)
            acc[...] += dot_nt(jnp.concatenate([high, low], axis=0), hhi[zc])
            acc2[...] += dot_nt(high, hlo[zc])
            gsrc[...] += gram_planes(block[:K], block[K:])
        for k in range(1, C):
            c_gram(t, k).start()
        total = acc[: 2 * K] + acc[2 * K :] + acc2[...]
        re = total[:K, :512] - total[K:, 512:]
        im = total[K:, :512] + total[:K, 512:]
        for q in range(4):
            even, odd = pack_pair(re[:, 128 * q : 128 * q + 128], im[:, 128 * q : 128 * q + 128])
            pk[2 * q], pk[2 * q + 1] = even, odd
        for k in range(1, C):
            c_part(k).start()

        @pl.when(c == z)
        def _():
            for q in range(4):
                chunk = ybuf.at[2 * x + q // 2]
                part_lanes = slice((q % 2) * 128, (q % 2) * 128 + 128)
                even, odd = pack_pair(chunk[:K, part_lanes], chunk[K:, part_lanes])
                scat[t, 2 * q], scat[t, 2 * q + 1] = even, odd
            for k in range(1, C):
                c_scatter(t, k).start()
            ypc[t] = scat[t, c]

    def row_sum():
        total = pk[c]
        for k in range(1, C):
            c_part(k).wait_recv()
            total = total + rsy[k]
        return total

    def c_factor(t):
        total = gsrc[...]
        for k in range(1, C):
            c_gram(t, k).wait_recv()
            total = total + gyc[t, k]
        return inverse_factor(total * (1.0 / N))

    def scattered(t):
        @pl.when(c != z)
        def _():
            c_scatter(t, 1).wait_recv()

        return ypc[t]

    def row_sent(t):
        for k in range(1, C):
            c_part(k).wait_send()
            c_gram(t, k).wait_send()

        @pl.when(c == z)
        def _():
            for k in range(1, C):
                c_scatter(t, k).wait_send()

    v_re, v_im = initial[0], initial[1]
    set_left(v_re, v_im)
    column_product(True, False)
    pl.semaphore_wait(barrier, len(partners))
    loop(Z, send_parts)
    for q in range(4):
        even, odd = pack_pair(v_re[:, 128 * q : 128 * q + 128], v_im[:, 128 * q : 128 * q + 128])
        pk[2 * q], pk[2 * q + 1] = even, odd
    v_piece = pk[c]
    column_mix()
    column_sum()
    column_gather(iter(()))
    row_product(0, None)
    z2_piece = row_sum()
    gy[c] = z2_piece

    def c_whole(k, src):
        return remote(gy.at[src], gy.at[src], agy_s.at[k], agy_r.at[k], at_c(k))

    for k in range(1, C):
        c_whole(k, c).start()
    inv1 = c_factor(0)
    column_sent()
    for k in range(1, C):
        c_whole(k, (c + C - k) & 7).wait_recv()
    pairs = [unpack_pair(gy[2 * q], gy[2 * q + 1]) for q in range(4)]
    block = jnp.concatenate(
        [jnp.concatenate([pair[p] for pair in pairs], axis=1) for p in range(2)], axis=0
    )
    block = dot(embedded(inv1), block, HIGH)
    set_left(block[:K], block[K:])
    column_product(False, True)
    gxs[...] = gram_planes(block[:K], block[K:])

    def x_gram(j):
        return remote(gxs, gx.at[j], gx_s.at[j], gx_r.at[j], at_x(j))

    def z_gram(o):
        return remote(gzs, gz.at[o], gz_s.at[o], gz_r.at[o], at_z(o))

    for j in range(1, X):
        x_gram(j).start()
    column_mix()
    row_sent(0)
    y2_piece = apply_packed(inv1, z2_piece)
    y1_piece = scattered(0)
    psrc[:K] = gram_packed(v_piece, y1_piece)
    psrc[K : 2 * K] = conj_apply_packed(inv1, gram_packed(y1_piece, y2_piece))
    total = gxs[...]
    for j in range(1, X):
        x_gram(j).wait_recv()
        total = total + gx[j]
    gzs[...] = total
    for o in range(1, Z):
        z_gram(o).start()
    column_sum()
    total = gzs[...]
    for o in range(1, Z):
        z_gram(o).wait_recv()
        total = total + gz[o]
    inv2 = []
    column_gather(factor_steps(total * (1.0 / N), inv2))
    inv2 = inv2[0]
    row_product(1, embedded(inv2))
    z4_piece = row_sum()


    def g_c(k):
        return remote(g4.at[0], g4y.at[k], g4y_s.at[k], g4y_r.at[k], at_c(k))

    def g_x(j):
        return remote(g4.at[1], g4x.at[j], g4x_s.at[j], g4x_r.at[j], at_x(j))

    def g_z(o):
        return remote(g4.at[2], g4z.at[o], g4z_s.at[o], g4z_r.at[o], at_z(o))

    def slab(shift):
        return pl.ds(pl.multiple_of(((c + shift) & 7) * RB, 8), RB)

    def p_c(k):
        return remote(psrc.at[slab(k)], py.at[k], py_s.at[k], py_r.at[k], at_c(k))

    def p_x(j):
        return remote(px.at[0], px.at[j], px_s.at[j], px_r.at[j], at_x(j))

    def p_z(o):
        return remote(pz.at[0], pz.at[o], pz_s.at[o], pz_r.at[o], at_z(o))

    def p_all(k, shift):
        return remote(pall.at[slab(shift)], pall.at[slab(shift)], pa_s.at[k], pa_r.at[k], at_c(k))

    def added(total, n, copy, slots):
        for i in range(1, n):
            copy(i).wait_recv()
            total = total + slots[i]
        return total

    gram = gram_packed(z4_piece, z4_piece)
    g4[0] = gram
    for k in range(1, C):
        g_c(k).start()
    inv3 = c_factor(1)
    gram = both_sides(inv3, added(gram, C, g_c, g4y))
    g4[1] = gram
    for j in range(1, X):
        g_x(j).start()
    y4_piece = apply_packed(inv3, z4_piece)
    y3_piece = scattered(1)
    psrc[2 * K : 3 * K] = conj_apply_packed(inv2, gram_packed(y2_piece, y3_piece))
    psrc[3 * K :] = conj_apply_packed(inv3, gram_packed(y3_piece, y4_piece))
    for k in range(1, C):
        p_c(k).start()
    gram = added(gram, X, g_x, g4x)
    g4[2] = gram
    for o in range(1, Z):
        g_z(o).start()
    px[0] = added(psrc[slab(0)], C, p_c, py)
    for j in range(1, X):
        p_x(j).start()
    pz[0] = added(px[0], X, p_x, px)
    for o in range(1, Z):
        p_z(o).start()
    gram = added(gram, Z, g_z, g4z)
    value = []
    steps = factor_steps(gram * (1.0 / N), value)
    for _ in range(3):
        next(steps)
    pall[slab(0)] = added(pz[0], Z, p_z, pz) * (1.0 / N)
    for k in range(1, C):
        p_all(k, 0).start()
    for _ in steps:
        pass
    value = apply_packed(value[0], y4_piece)
    basis[0] = value[:, :64]
    basis[1] = pltpu.roll(value, 64, 1)[:, :64]
    for k in range(1, C):
        p_all(k, C - k).wait_recv()
    for t in range(ITERS):
        value = pall[K * t : K * t + K]
        ritz[t, 0] = value[:, :K]
        ritz[t, 1] = pltpu.roll(value, 64, 1)[:, :K]

    column_sent()
    row_sent(1)
    for k in range(1, C):
        c_whole(k, c).wait_send()
        g_c(k).wait_send()
        p_c(k).wait_send()
        p_all(k, 0).wait_send()
    for j in range(1, X):
        x_gram(j).wait_send()
        g_x(j).wait_send()
        p_x(j).wait_send()
    for o in range(1, Z):
        z_gram(o).wait_send()
        g_z(o).wait_send()
        p_z(o).wait_send()


def solution(mesh):
    dma = pltpu.SemaphoreType.DMA
    packed, piece = (K, 128), (RB, 128)
    scratch = [
        pltpu.VMEM((Z, 2, 512, CH), F32),
        pltpu.VMEM((Z, 1024, CH), BF16),
        pltpu.VMEM((Z, 1024, CH), BF16),
        pltpu.VMEM((4 * K, 1024), BF16),
        pltpu.VMEM((Z, 2 * K, CH), F32),
        pltpu.VMEM((3, Z, RB, CH), F32),
        pltpu.VMEM((Z, RB, CH), F32),
        pltpu.VMEM((Z, RB, CH), F32),
        pltpu.VMEM((Z, RB, CH), F32),
        pltpu.VMEM((Z, 2 * K, CH), F32),
        pltpu.VMEM((Z, 2 * K, CH), F32),
        pltpu.VMEM((4 * K, 1024), F32),
        pltpu.VMEM((2 * K, 1024), F32),
        pltpu.VMEM((C, *packed), F32),
        pltpu.VMEM((C, *packed), F32),
        pltpu.VMEM((C, *packed), F32),
        pltpu.VMEM((2, C, *packed), F32),
        pltpu.VMEM((2, *packed), F32),
        pltpu.VMEM(packed, F32),
        pltpu.VMEM((2, C, *packed), F32),
        pltpu.VMEM(packed, F32),
        pltpu.VMEM((X, *packed), F32),
        pltpu.VMEM(packed, F32),
        pltpu.VMEM((Z, *packed), F32),
        pltpu.VMEM((3, *packed), F32),
        pltpu.VMEM((C, *packed), F32),
        pltpu.VMEM((X, *packed), F32),
        pltpu.VMEM((Z, *packed), F32),
        pltpu.VMEM((4 * K, 128), F32),
        pltpu.VMEM((C, *piece), F32),
        pltpu.VMEM((X, *piece), F32),
        pltpu.VMEM((Z, *piece), F32),
        pltpu.VMEM((4 * K, 128), F32),
        dma((Z,)),
        dma((3, Z)), dma((3, Z)), dma((Z,)), dma((Z,)),
        dma((Z,)), dma((Z,)), dma((3, Z)), dma((3, Z)),
        dma((C,)), dma((C,)), dma((C,)), dma((C,)),
        dma((2, C)), dma((2,)), dma((2, C)), dma((2, C)),
        dma((X,)), dma((X,)), dma((Z,)), dma((Z,)),
        dma((C,)), dma((C,)), dma((X,)), dma((X,)), dma((Z,)), dma((Z,)),
        dma((C,)), dma((C,)), dma((X,)), dma((X,)), dma((Z,)), dma((Z,)), dma((C,)), dma((C,)),
    ]
    vmem = pl.BlockSpec(memory_space=pltpu.VMEM)

    def body(coupling, initial):
        return pl.pallas_call(
            kernel,
            name="subspace",
            out_shape=(
                jax.ShapeDtypeStruct((2, K, 64), F32),
                jax.ShapeDtypeStruct((ITERS, 2, K, K), F32),
            ),
            in_specs=[pl.BlockSpec(memory_space=pl.ANY), vmem],
            out_specs=(vmem, vmem),
            scratch_shapes=scratch,
            compiler_params=pltpu.CompilerParams(
                collective_id=0, has_side_effects=True, vmem_limit_bytes=56 * 1024 * 1024
            ),
        )(coupling, initial)

    return jax.shard_map(
        body,
        mesh=mesh,
        in_specs=(P(None, "rows", "cols"), P(None, None, "rows")),
        out_specs=(P(None, None, ("rows", "cols")), P()),
        check_vma=False,
    )
```

```python
import jax
import jax.numpy as jnp
from jax import lax
from jax.experimental import pallas as pl
from jax.experimental.pallas import tpu as pltpu
from jax.sharding import PartitionSpec as P

N = 16384
K = 48
ITERS = 4
X, Z, C = 4, 8, 8
CH = 256
RB = 2 * K // X
F32, BF16 = jnp.float32, jnp.bfloat16
MESH = pl.DeviceIdType.MESH
NT = (((1,), (1,)), ((), ()))


def dot(a, b):
    return jnp.dot(a, b, preferred_element_type=F32)


def dot_nt(a, b):
    return lax.dot_general(a, b, NT, preferred_element_type=F32)


def split(value):
    high = value.astype(BF16)
    return high, (value - high.astype(F32)).astype(BF16)


def in_parts(product, a, b):
    (ah, al), (bh, bl) = split(a), split(b)
    return product(ah, bh) + (product(ah, bl) + product(al, bh))


def lanes(shape):
    return lax.broadcasted_iota(jnp.int32, shape, 1)


def turned(packed):
    rolled = pltpu.roll(packed, 64, 1)
    return jnp.where(lanes(packed.shape) < 64, rolled, -rolled)


def stacked_rows(first, second):
    gap = jnp.zeros((64 - K, first.shape[1]), first.dtype)
    return jnp.concatenate([first, gap, second, gap], axis=0)


def gram_packed(left, right):
    return in_parts(dot_nt, left, stacked_rows(right, turned(right)))


def gram_planes(re, im):
    return in_parts(dot_nt, re, stacked_rows(re, im)) + in_parts(dot_nt, im, stacked_rows(im, -re))


def planes_of(packed):
    low = lanes(packed.shape) < 64
    return jnp.where(low, packed, 0.0), jnp.where(low, pltpu.roll(packed, 64, 1), 0.0)


def apply_packed(matrix, packed):
    re, im = planes_of(matrix)
    return in_parts(dot, re[:, :K], packed) - in_parts(dot, im[:, :K], turned(packed))


def conj_apply_packed(matrix, packed):
    re, im = planes_of(matrix)
    return in_parts(dot, re[:, :K], packed) + in_parts(dot, im[:, :K], turned(packed))


def embedded(matrix):
    re, im = planes_of(matrix)
    upper = re - pltpu.roll(im, K, 1)
    lower = im + pltpu.roll(re, K, 1)
    return jnp.concatenate([upper, lower], axis=0)[:, : 2 * K]


def factor_start(gram):
    lane = lanes((K, 128))
    row = lax.broadcasted_iota(jnp.int32, (K, 128), 0)
    low = lane < 64
    re = jnp.where(low, gram, jnp.where(lane - 64 == row, 1.0, 0.0))
    im = jnp.where(low, pltpu.roll(gram, 64, 1), 0.0)
    return tuple(plane[t : t + 8] for plane in (re, im) for t in range(0, K, 8))


def factor_block(block, tiles):
    n = K // 8
    re, im = list(tiles[:n]), list(tiles[n:])
    below = lax.broadcasted_iota(jnp.int32, (8, 1), 0)
    open_tile = [None] + [jnp.where(block + t < n, 1.0, 0.0) for t in range(1, n)]
    for s in range(8):
        row_re, row_im = re[0][s : s + 1], im[0][s : s + 1]
        inv = 1.0 / row_re[:, s : s + 1]
        for t in range(n):
            if t == 0:
                m_re = jnp.where(below > s, re[t][:, s : s + 1] * inv, 0.0)
                m_im = jnp.where(below > s, im[t][:, s : s + 1] * inv, 0.0)
            else:
                m_re = re[t][:, s : s + 1] * (inv * open_tile[t])
                m_im = im[t][:, s : s + 1] * (inv * open_tile[t])
            re[t], im[t] = (
                re[t] - (m_re * row_re - m_im * row_im),
                im[t] - (m_re * row_im + m_im * row_re),
            )
    moved = [pltpu.roll(tile, 128 - 8, 1) for tile in re[1:] + re[:1] + im[1:] + im[:1]]
    return tuple(moved)


def factor_end(tiles):
    n = K // 8
    re = pltpu.roll(jnp.concatenate(tiles[:n], axis=0), K, 1)
    im = pltpu.roll(jnp.concatenate(tiles[n:], axis=0), K, 1)
    lane = lanes((K, 128))
    row = lax.broadcasted_iota(jnp.int32, (K, 128), 0)
    pivot = jnp.sum(jnp.where(lane == row, re, 0.0), axis=1, keepdims=True)
    scale = 1.0 / jnp.sqrt(pivot)
    return jnp.where(lane < 64, pltpu.roll(re, 64, 1), im) * scale


def inverse_factor(gram):
    return factor_end(lax.fori_loop(0, K // 8, factor_block, factor_start(gram)))


def both_sides(matrix, packed):
    left = conj_apply_packed(matrix, packed)
    low = lanes(matrix.shape) < 64
    return in_parts(dot_nt, left, stacked_rows(jnp.where(low, matrix, -matrix), pltpu.roll(matrix, 64, 1)))


def pack_pair(re, im):
    low = lanes(re.shape) < 64
    even = jnp.where(low, re, pltpu.roll(im, 64, 1))
    odd = jnp.where(low, pltpu.roll(re, 64, 1), im)
    return even, odd


def pack_hermitian(first, second):
    lane, row = lanes(first.shape), lax.broadcasted_iota(jnp.int32, first.shape, 0)
    one = jnp.where(lane >= row, first, pltpu.roll(first, 64, 1))
    two = jnp.where(lane - 64 >= row, pltpu.roll(second, 64, 1), second)
    return jnp.where(lane < 64, one, two)


def unpack_hermitian(both):
    lane, row = lanes((K, 128)), lax.broadcasted_iota(jnp.int32, (K, 128), 0)
    column = lane & 63
    flipped = jnp.concatenate([both, jnp.zeros((128 - K, 128), F32)], axis=0).T
    other = jnp.where(lane < 64, flipped[:K], pltpu.roll(flipped[64 : 64 + K], 64, 1))
    re = jnp.where(column >= row, both, other)
    im = jnp.where(column < row, both, jnp.where(column > row, -other, 0.0))
    low = lane < 64
    return jnp.where(low, re, pltpu.roll(im, 64, 1)), jnp.where(low, pltpu.roll(re, 64, 1), im)


def unpack_pair(even, odd):
    low = lanes(even.shape) < 64
    re = jnp.where(low, even, pltpu.roll(odd, 64, 1))
    im = jnp.where(low, pltpu.roll(even, 64, 1), odd)
    return re, im


def far_first(k):
    return 4 + (k >> 1) * (1 - (k & 1)) - ((k + 1) >> 1) * (k & 1)


def near_first(k):
    return far_first(7 - k) & 7


def kernel(coupling, initial, basis, ritz, *scratch):
    (
        stage, hhi, hlo, lhs, part, rsx, red, rsz, gath, ybuf, acc, acc2,
        pk, rsy, gy, scat, ypc, gsrc, gyc, gxs, gx, gzs, gz,
        g4, g4y, g4x, g4z, psrc, py, px, pz, pall,
        hsem, rsx_s, rsx_r, rsz_s, rsz_r, agz_s, agz_r, agx_s, agx_r,
        rsy_s, rsy_r, agy_s, agy_r, sc_s, sc_r, gyc_s, gyc_r, gx_s, gx_r, gz_s, gz_r,
        g4y_s, g4y_r, g4x_s, g4x_r, g4z_s, g4z_r, py_s, py_r, px_s, px_r, pz_s, pz_r, pa_s, pa_r,
    ) = scratch
    r, c = lax.axis_index("rows"), lax.axis_index("cols")
    z, x = r >> 2, r & 3

    def at_x(j):
        return (z * X + ((x + j) & 3), c)

    def at_z(o):
        return (((z + o) & 7) * X + x, c)

    def at_c(k):
        return (r, (c + k) & 7)

    def remote(src, dst, send, recv, dev):
        return pltpu.make_async_remote_copy(
            src_ref=src, dst_ref=dst, send_sem=send, recv_sem=recv,
            device_id=dev, device_id_type=MESH,
        )

    def loop(n, f):
        def step(i, carry):
            f(i)
            return carry

        lax.fori_loop(0, n, step, 0)

    def rows_of(j):
        return pl.ds(pl.multiple_of(((x + j) & 3) * RB, 8), RB)

    def far(k):
        return (z + far_first(k)) & 7

    def near(k):
        return (z + 8 - near_first(k)) & 7

    def load(k):
        columns = pl.ds(pl.multiple_of(far(k) * CH, CH), CH)
        return pltpu.make_async_copy(coupling.at[:, :, columns], stage.at[far(k)], hsem.at[far(k)])

    loop(Z, lambda k: load(k).start())

    barrier = pltpu.get_barrier_semaphore()
    partners = [at_x(j) for j in range(1, X)] + [at_z(o) for o in range(1, Z)]
    partners += [at_c(k) for k in range(1, C)]
    for dev in partners:
        pl.semaphore_signal(barrier, inc=1, device_id=dev, device_id_type=MESH)

    def set_left(re, im):
        top = jnp.concatenate([re, im], axis=1)
        bottom = jnp.concatenate([im, -re], axis=1)
        high, low = split(jnp.concatenate([top, bottom], axis=0))
        lhs[...] = jnp.concatenate([high, low], axis=0)


    def x_part(j, zc):
        return remote(
            part.at[zc, rows_of(j)], rsx.at[j - 1, zc], rsx_s.at[j - 1, zc], rsx_r.at[j - 1, zc], at_x(j)
        )

    def z_part(k):
        o = far_first(k)
        return remote(red.at[far(k)], rsz.at[o], rsz_s.at[o], rsz_r.at[o], at_z(o))

    def send_parts(k):
        for j in range(1, X):
            x_part(j, far(k)).start()

    def column_product(load_first, send):
        def chunk(k):
            zc = far(k)
            if load_first:
                load(k).wait()
                for t in range(0, 1024, 128):
                    high, low = split(stage[zc, t // 512, t % 512 : t % 512 + 128])
                    hhi[zc, t : t + 128] = high
                    hlo[zc, t : t + 128] = low
            both = dot(lhs[...], hhi[zc])
            part[zc] = both[: 2 * K] + both[2 * K :] + dot(lhs[: 2 * K], hlo[zc])
            if send:
                send_parts(k)

        loop(Z, chunk)

    def column_sum():
        def chunk(k):
            zc = far(k)
            total = part[zc, rows_of(0)]
            for j in range(1, X):
                x_part(j, zc).wait_recv()
                total = total + rsx[j - 1, zc]
            red[zc] = total

            @pl.when(k < Z - 1)
            def _():
                z_part(k).start()

        loop(Z, chunk)


    def z_whole(o, zc):
        block = gath.at[zc, rows_of(0)]
        return remote(block, block, agz_s.at[o], agz_r.at[o], at_z(o))

    def x_whole(j, zc, shift):
        block = gath.at[zc, rows_of(shift)]
        return remote(block, block, agx_s.at[j - 1, zc], agx_r.at[j - 1, zc], at_x(j))

    def column_gather(tiles):
        def last(k, total):
            z_part(k).wait_recv()
            return total + rsz[far_first(k)]

        gath[z, rows_of(0)] = lax.fori_loop(0, Z - 1, last, red[z])
        loop(Z - 1, lambda k: z_whole(far_first(k), z).start())
        for j in range(1, X):
            x_whole(j, z, 0).start()

        def forward(k):
            z_whole(near_first(k), near(k)).wait_recv()
            for j in range(1, X):
                x_whole(j, near(k), 0).start()

        def step(k, tiles):
            tiles = factor_block(k, tiles)
            forward(k + 1)
            return tiles

        if tiles is None:
            loop(Z - 1, lambda k: forward(k + 1))
            return None
        tiles = lax.fori_loop(0, K // 8, step, tiles)
        forward(Z - 1)
        return factor_end(tiles)

    def column_sent():
        def chunk(k):
            for j in range(1, X):
                x_part(j, k).wait_send()
                x_whole(j, k, 0).wait_send()

            @pl.when(k < Z - 1)
            def _():
                z_part(k).wait_send()
                z_whole(far_first(k), z).wait_send()

        loop(Z, chunk)

    def c_gram(t, k):
        return remote(gsrc, gyc.at[t, k], gyc_s.at[t, k], gyc_r.at[t, k], at_c(k))

    def c_scatter(t, k):
        return remote(scat.at[t, (c + k) & 7], ypc.at[t], sc_s.at[t, k], sc_r.at[t], at_c(k))

    def c_part(k):
        return remote(pk.at[(c + k) & 7], rsy.at[k], rsy_s.at[k], rsy_r.at[k], at_c(k))

    def row_product(t, factor):
        acc[...] = jnp.zeros_like(acc)
        acc2[...] = jnp.zeros_like(acc2)
        gsrc[...] = jnp.zeros_like(gsrc)

        def receive(k):
            zc = near(k)
            for j in range(1, X):
                x_whole(j, zc, X - j).wait_recv()
            block = gath[zc]
            if factor is not None:
                block = in_parts(dot, factor, block)
            ybuf[zc] = block
            high, low = split(block)
            acc[...] += dot_nt(jnp.concatenate([high, low], axis=0), hhi[zc])
            acc2[...] += dot_nt(high, hlo[zc])
            gsrc[...] += gram_planes(block[:K], block[K:])

        loop(Z, receive)
        for k in range(1, C):
            c_gram(t, k).start()
        total = acc[: 2 * K] + acc[2 * K :] + acc2[...]
        re = total[:K, :512] - total[K:, 512:]
        im = total[K:, :512] + total[:K, 512:]
        for q in range(4):
            even, odd = pack_pair(re[:, 128 * q : 128 * q + 128], im[:, 128 * q : 128 * q + 128])
            pk[2 * q], pk[2 * q + 1] = even, odd
        for k in range(1, C):
            c_part(k).start()

        @pl.when(c == z)
        def _():
            for q in range(4):
                chunk = ybuf.at[2 * x + q // 2]
                part_lanes = slice((q % 2) * 128, (q % 2) * 128 + 128)
                even, odd = pack_pair(chunk[:K, part_lanes], chunk[K:, part_lanes])
                scat[t, 2 * q], scat[t, 2 * q + 1] = even, odd
            for k in range(1, C):
                c_scatter(t, k).start()
            ypc[t] = scat[t, c]

    def row_sum():
        total = pk[c]
        for k in range(1, C):
            c_part(k).wait_recv()
            total = total + rsy[k]
        return total

    def c_factor(t):
        total = gsrc[...]
        for k in range(1, C):
            c_gram(t, k).wait_recv()
            total = total + gyc[t, k]
        return inverse_factor(total * (1.0 / N))

    def scattered(t):
        @pl.when(c != z)
        def _():
            c_scatter(t, 1).wait_recv()

        return ypc[t]

    def row_sent(t):
        for k in range(1, C):
            c_part(k).wait_send()
            c_gram(t, k).wait_send()

        @pl.when(c == z)
        def _():
            for k in range(1, C):
                c_scatter(t, k).wait_send()

    v_re, v_im = initial[0], initial[1]
    set_left(v_re, v_im)
    pl.semaphore_wait(barrier, len(partners))
    column_product(True, True)
    for q in range(4):
        even, odd = pack_pair(v_re[:, 128 * q : 128 * q + 128], v_im[:, 128 * q : 128 * q + 128])
        pk[2 * q], pk[2 * q + 1] = even, odd
    v_piece = pk[c]
    column_sum()
    column_gather(None)
    row_product(0, None)
    z2_piece = row_sum()
    gy[c] = z2_piece

    def c_whole(k, src):
        return remote(gy.at[src], gy.at[src], agy_s.at[k], agy_r.at[k], at_c(k))

    for k in range(1, C):
        c_whole(k, c).start()
    inv1 = c_factor(0)
    column_sent()
    for k in range(1, C):
        c_whole(k, (c + C - k) & 7).wait_recv()
    pairs = [unpack_pair(gy[2 * q], gy[2 * q + 1]) for q in range(4)]
    block = jnp.concatenate(
        [jnp.concatenate([pair[p] for pair in pairs], axis=1) for p in range(2)], axis=0
    )
    block = in_parts(dot, embedded(inv1), block)
    set_left(block[:K], block[K:])
    gxs[...] = gram_planes(block[:K], block[K:])

    def x_gram(j):
        return remote(gxs, gx.at[j], gx_s.at[j], gx_r.at[j], at_x(j))

    def z_gram(o):
        return remote(gzs, gz.at[o], gz_s.at[o], gz_r.at[o], at_z(o))

    for j in range(1, X):
        x_gram(j).start()
    column_product(False, True)
    total = gxs[...]
    for j in range(1, X):
        x_gram(j).wait_recv()
        total = total + gx[j]
    gzs[...] = total
    for o in range(1, Z):
        z_gram(o).start()
    row_sent(0)
    y2_piece = apply_packed(inv1, z2_piece)
    y1_piece = scattered(0)
    psrc[:K] = gram_packed(v_piece, y1_piece)
    psrc[K : 2 * K] = conj_apply_packed(inv1, gram_packed(y1_piece, y2_piece))
    column_sum()
    total = gzs[...]
    for o in range(1, Z):
        z_gram(o).wait_recv()
        total = total + gz[o]
    inv2 = column_gather(factor_start(total * (1.0 / N)))
    row_product(1, embedded(inv2))
    z4_piece = row_sum()


    def g_c(k):
        return remote(g4.at[0], g4y.at[k], g4y_s.at[k], g4y_r.at[k], at_c(k))

    def g_x(j):
        return remote(g4.at[1], g4x.at[j], g4x_s.at[j], g4x_r.at[j], at_x(j))

    def g_z(o):
        return remote(g4.at[2], g4z.at[o], g4z_s.at[o], g4z_r.at[o], at_z(o))

    def slab(shift):
        return pl.ds(pl.multiple_of(((c + shift) & 7) * RB, 8), RB)

    def p_c(k):
        return remote(psrc.at[slab(k)], py.at[k], py_s.at[k], py_r.at[k], at_c(k))

    def p_x(j):
        return remote(px.at[0], px.at[j], px_s.at[j], px_r.at[j], at_x(j))

    def p_z(o):
        return remote(pz.at[0], pz.at[o], pz_s.at[o], pz_r.at[o], at_z(o))

    def p_all(k, shift):
        return remote(pall.at[slab(shift)], pall.at[slab(shift)], pa_s.at[k], pa_r.at[k], at_c(k))

    def added(total, n, copy, slots):
        for i in range(1, n):
            copy(i).wait_recv()
            total = total + slots[i]
        return total

    y3_piece = scattered(1)
    both = pack_hermitian(gram_packed(z4_piece, z4_piece), gram_packed(y3_piece, z4_piece))
    g4[0] = both
    for k in range(1, C):
        g_c(k).start()
    psrc[2 * K : 3 * K] = conj_apply_packed(inv2, gram_packed(y2_piece, y3_piece))
    psrc[3 * K :] = jnp.zeros((K, 128), F32)
    for k in range(1, C):
        p_c(k).start()
    inv3 = c_factor(1)
    y4_piece = apply_packed(inv3, z4_piece)
    both = added(both, C, g_c, g4y)
    g4[1] = both
    for j in range(1, X):
        g_x(j).start()
    px[0] = added(psrc[slab(0)], C, p_c, py)
    for j in range(1, X):
        p_x(j).start()
    both = added(both, X, g_x, g4x)
    g4[2] = both
    for o in range(1, Z):
        g_z(o).start()
    pz[0] = added(px[0], X, p_x, px)
    for o in range(1, Z):
        p_z(o).start()
    both = added(both, Z, g_z, g4z) * (1.0 / N)
    pall[slab(0)] = added(pz[0], Z, p_z, pz) * (1.0 / N)
    for k in range(1, C):
        p_all(k, 0).start()
    gram, projection = unpack_hermitian(both)
    value = apply_packed(inverse_factor(both_sides(inv3, gram)), y4_piece)
    basis[0] = value[:, :64]
    basis[1] = pltpu.roll(value, 64, 1)[:, :64]
    for k in range(1, C):
        p_all(k, C - k).wait_recv()
    for t in range(ITERS):
        value = pall[K * t : K * t + K] if t < ITERS - 1 else both_sides(inv3, projection)
        ritz[t, 0] = value[:, :K]
        ritz[t, 1] = pltpu.roll(value, 64, 1)[:, :K]

    column_sent()
    row_sent(1)
    for k in range(1, C):
        c_whole(k, c).wait_send()
        g_c(k).wait_send()
        p_c(k).wait_send()
        p_all(k, 0).wait_send()
    for j in range(1, X):
        x_gram(j).wait_send()
        g_x(j).wait_send()
        p_x(j).wait_send()
    for o in range(1, Z):
        z_gram(o).wait_send()
        g_z(o).wait_send()
        p_z(o).wait_send()


def solution(mesh):
    dma = pltpu.SemaphoreType.DMA
    packed, piece = (K, 128), (RB, 128)
    scratch = [
        pltpu.VMEM((Z, 2, 512, CH), F32),
        pltpu.VMEM((Z, 1024, CH), BF16),
        pltpu.VMEM((Z, 1024, CH), BF16),
        pltpu.VMEM((4 * K, 1024), BF16),
        pltpu.VMEM((Z, 2 * K, CH), F32),
        pltpu.VMEM((3, Z, RB, CH), F32),
        pltpu.VMEM((Z, RB, CH), F32),
        pltpu.VMEM((Z, RB, CH), F32),
        pltpu.VMEM((Z, 2 * K, CH), F32),
        pltpu.VMEM((Z, 2 * K, CH), F32),
        pltpu.VMEM((4 * K, 1024), F32),
        pltpu.VMEM((2 * K, 1024), F32),
        pltpu.VMEM((C, *packed), F32),
        pltpu.VMEM((C, *packed), F32),
        pltpu.VMEM((C, *packed), F32),
        pltpu.VMEM((2, C, *packed), F32),
        pltpu.VMEM((2, *packed), F32),
        pltpu.VMEM(packed, F32),
        pltpu.VMEM((2, C, *packed), F32),
        pltpu.VMEM(packed, F32),
        pltpu.VMEM((X, *packed), F32),
        pltpu.VMEM(packed, F32),
        pltpu.VMEM((Z, *packed), F32),
        pltpu.VMEM((3, *packed), F32),
        pltpu.VMEM((C, *packed), F32),
        pltpu.VMEM((X, *packed), F32),
        pltpu.VMEM((Z, *packed), F32),
        pltpu.VMEM((4 * K, 128), F32),
        pltpu.VMEM((C, *piece), F32),
        pltpu.VMEM((X, *piece), F32),
        pltpu.VMEM((Z, *piece), F32),
        pltpu.VMEM((4 * K, 128), F32),
        dma((Z,)),
        dma((3, Z)), dma((3, Z)), dma((Z,)), dma((Z,)),
        dma((Z,)), dma((Z,)), dma((3, Z)), dma((3, Z)),
        dma((C,)), dma((C,)), dma((C,)), dma((C,)),
        dma((2, C)), dma((2,)), dma((2, C)), dma((2, C)),
        dma((X,)), dma((X,)), dma((Z,)), dma((Z,)),
        dma((C,)), dma((C,)), dma((X,)), dma((X,)), dma((Z,)), dma((Z,)),
        dma((C,)), dma((C,)), dma((X,)), dma((X,)), dma((Z,)), dma((Z,)), dma((C,)), dma((C,)),
    ]
    vmem = pl.BlockSpec(memory_space=pltpu.VMEM)

    def body(coupling, initial):
        return pl.pallas_call(
            kernel,
            name="subspace",
            out_shape=(
                jax.ShapeDtypeStruct((2, K, 64), F32),
                jax.ShapeDtypeStruct((ITERS, 2, K, K), F32),
            ),
            in_specs=[pl.BlockSpec(memory_space=pl.ANY), vmem],
            out_specs=(vmem, vmem),
            scratch_shapes=scratch,
            compiler_params=pltpu.CompilerParams(
                collective_id=0, has_side_effects=True, vmem_limit_bytes=56 * 1024 * 1024
            ),
        )(coupling, initial)

    return jax.shard_map(
        body,
        mesh=mesh,
        in_specs=(P(None, "rows", "cols"), P(None, None, "rows")),
        out_specs=(P(None, None, ("rows", "cols")), P()),
        check_vma=False,
    )
```

```python
import jax
import jax.numpy as jnp
from jax import lax
from jax.experimental import pallas as pl
from jax.experimental.pallas import tpu as pltpu
from jax.sharding import PartitionSpec as P

N = 16384
K = 48
ITERS = 4
X, Z, C = 4, 8, 8
CH = 256
RB = 2 * K // X
F32, BF16 = jnp.float32, jnp.bfloat16
MESH = pl.DeviceIdType.MESH
NT = (((1,), (1,)), ((), ()))


def dot(a, b):
    return jnp.dot(a, b, preferred_element_type=F32)


def dot_nt(a, b):
    return lax.dot_general(a, b, NT, preferred_element_type=F32)


def split(value):
    high = value.astype(BF16)
    return high, (value - high.astype(F32)).astype(BF16)


def in_parts(product, a, b):
    (ah, al), (bh, bl) = split(a), split(b)
    return product(ah, bh) + (product(ah, bl) + product(al, bh))


def lanes(shape):
    return lax.broadcasted_iota(jnp.int32, shape, 1)


def turned(packed):
    rolled = pltpu.roll(packed, 64, 1)
    return jnp.where(lanes(packed.shape) < 64, rolled, -rolled)


def stacked_rows(first, second):
    gap = jnp.zeros((64 - K, first.shape[1]), first.dtype)
    return jnp.concatenate([first, gap, second, gap], axis=0)


def gram_packed(left, right):
    return in_parts(dot_nt, left, stacked_rows(right, turned(right)))


def gram_planes(re, im):
    return in_parts(dot_nt, re, stacked_rows(re, im)) + in_parts(dot_nt, im, stacked_rows(im, -re))


def planes_of(packed):
    low = lanes(packed.shape) < 64
    return jnp.where(low, packed, 0.0), jnp.where(low, pltpu.roll(packed, 64, 1), 0.0)


def apply_packed(matrix, packed):
    re, im = planes_of(matrix)
    return in_parts(dot, re[:, :K], packed) - in_parts(dot, im[:, :K], turned(packed))


def conj_apply_packed(matrix, packed):
    re, im = planes_of(matrix)
    return in_parts(dot, re[:, :K], packed) + in_parts(dot, im[:, :K], turned(packed))


def embedded(matrix):
    re, im = planes_of(matrix)
    upper = re - pltpu.roll(im, K, 1)
    lower = im + pltpu.roll(re, K, 1)
    return jnp.concatenate([upper, lower], axis=0)[:, : 2 * K]


def factor_start(gram):
    lane = lanes((K, 128))
    row = lax.broadcasted_iota(jnp.int32, (K, 128), 0)
    low = lane < 64
    re = jnp.where(low, gram, jnp.where(lane - 64 == row, 1.0, 0.0))
    im = jnp.where(low, pltpu.roll(gram, 64, 1), 0.0)
    return tuple(plane[t : t + 8] for plane in (re, im) for t in range(0, K, 8))


def factor_block(block, tiles):
    n = K // 8
    re, im = list(tiles[:n]), list(tiles[n:])
    below = lax.broadcasted_iota(jnp.int32, (8, 1), 0)
    open_tile = [None] + [jnp.where(block + t < n, 1.0, 0.0) for t in range(1, n)]
    for s in range(8):
        row_re, row_im = re[0][s : s + 1], im[0][s : s + 1]
        inv = 1.0 / row_re[:, s : s + 1]
        for t in range(n):
            if t == 0:
                m_re = jnp.where(below > s, re[t][:, s : s + 1] * inv, 0.0)
                m_im = jnp.where(below > s, im[t][:, s : s + 1] * inv, 0.0)
            else:
                m_re = re[t][:, s : s + 1] * (inv * open_tile[t])
                m_im = im[t][:, s : s + 1] * (inv * open_tile[t])
            re[t], im[t] = (
                re[t] - (m_re * row_re - m_im * row_im),
                im[t] - (m_re * row_im + m_im * row_re),
            )
    moved = [pltpu.roll(tile, 128 - 8, 1) for tile in re[1:] + re[:1] + im[1:] + im[:1]]
    return tuple(moved)


def factor_end(tiles):
    n = K // 8
    re = pltpu.roll(jnp.concatenate(tiles[:n], axis=0), K, 1)
    im = pltpu.roll(jnp.concatenate(tiles[n:], axis=0), K, 1)
    lane = lanes((K, 128))
    row = lax.broadcasted_iota(jnp.int32, (K, 128), 0)
    pivot = jnp.sum(jnp.where(lane == row, re, 0.0), axis=1, keepdims=True)
    scale = 1.0 / jnp.sqrt(pivot)
    return jnp.where(lane < 64, pltpu.roll(re, 64, 1), im) * scale


def inverse_factor(gram):
    return factor_end(lax.fori_loop(0, K // 8, factor_block, factor_start(gram)))


def both_sides(matrix, packed):
    left = conj_apply_packed(matrix, packed)
    low = lanes(matrix.shape) < 64
    return in_parts(dot_nt, left, stacked_rows(jnp.where(low, matrix, -matrix), pltpu.roll(matrix, 64, 1)))


def pack_pair(re, im):
    low = lanes(re.shape) < 64
    even = jnp.where(low, re, pltpu.roll(im, 64, 1))
    odd = jnp.where(low, pltpu.roll(re, 64, 1), im)
    return even, odd


def pack_triangle(packed):
    lane, row = lanes(packed.shape), lax.broadcasted_iota(jnp.int32, packed.shape, 0)
    one = jnp.where(lane >= row, packed, pltpu.roll(packed, 64, 1))
    return jnp.where(lane[:RB] < 64, one[:RB], pltpu.roll(one[RB:], 64, 1))


def unpack_triangle(half):
    low = lanes(half.shape) < 64
    upper = jnp.where(low, half, 0.0)
    lower = jnp.where(low, pltpu.roll(half, 64, 1), 0.0)
    tri = jnp.concatenate([upper, lower], axis=0)
    lane, row = lanes((K, 128)), lax.broadcasted_iota(jnp.int32, (K, 128), 0)
    other = jnp.concatenate([tri, jnp.zeros((128 - K, 128), F32)], axis=0).T[:K]
    re = jnp.where(lane >= row, tri, other)
    im = jnp.where(lane < row, tri, jnp.where(lane > row, -other, 0.0))
    return jnp.where(lane < 64, re, pltpu.roll(im, 64, 1))


def unpack_pair(even, odd):
    low = lanes(even.shape) < 64
    re = jnp.where(low, even, pltpu.roll(odd, 64, 1))
    im = jnp.where(low, pltpu.roll(even, 64, 1), odd)
    return re, im


def far_first(k):
    return 4 + (k >> 1) * (1 - (k & 1)) - ((k + 1) >> 1) * (k & 1)


def near_first(k):
    return far_first(7 - k) & 7


def kernel(coupling, initial, basis, ritz, *scratch):
    (
        stage, hhi, hlo, lhs, part, rsx, red, rsz, gath, ybuf, acc, acc2,
        pk, rsy, gy, scat, ypc, gsum, gsrc, gyc, gxs, gx, gzs, gz,
        g4, g4y, g4x, g4z, psrc, py, px, pz, pall,
        hsem, rsx_s, rsx_r, rsz_s, rsz_r, agz_s, agz_r, agx_s, agx_r,
        rsy_s, rsy_r, agy_s, agy_r, sc_s, sc_r, gyc_s, gyc_r, gx_s, gx_r, gz_s, gz_r,
        g4y_s, g4y_r, g4x_s, g4x_r, g4z_s, g4z_r, py_s, py_r, px_s, px_r, pz_s, pz_r, pa_s, pa_r,
    ) = scratch
    r, c = lax.axis_index("rows"), lax.axis_index("cols")
    z, x = r >> 2, r & 3

    def at_x(j):
        return (z * X + ((x + j) & 3), c)

    def at_z(o):
        return (((z + o) & 7) * X + x, c)

    def at_c(k):
        return (r, (c + k) & 7)

    def remote(src, dst, send, recv, dev):
        return pltpu.make_async_remote_copy(
            src_ref=src, dst_ref=dst, send_sem=send, recv_sem=recv,
            device_id=dev, device_id_type=MESH,
        )

    def loop(n, f):
        def step(i, carry):
            f(i)
            return carry

        lax.fori_loop(0, n, step, 0)

    def rows_of(j):
        return pl.ds(pl.multiple_of(((x + j) & 3) * RB, 8), RB)

    def far(k):
        return (z + far_first(k)) & 7

    def near(k):
        return (z + 8 - near_first(k)) & 7

    def load(k):
        columns = pl.ds(pl.multiple_of(far(k) * CH, CH), CH)
        return pltpu.make_async_copy(coupling.at[:, :, columns], stage.at[far(k)], hsem.at[far(k)])

    loop(Z, lambda k: load(k).start())

    barrier = pltpu.get_barrier_semaphore()
    partners = [at_x(j) for j in range(1, X)] + [at_z(o) for o in range(1, Z)]
    partners += [at_c(k) for k in range(1, C)]
    for dev in partners:
        pl.semaphore_signal(barrier, inc=1, device_id=dev, device_id_type=MESH)

    def set_left(re, im):
        top = jnp.concatenate([re, im], axis=1)
        bottom = jnp.concatenate([im, -re], axis=1)
        high, low = split(jnp.concatenate([top, bottom], axis=0))
        lhs[...] = jnp.concatenate([high, low], axis=0)


    def x_part(j, zc):
        return remote(
            part.at[zc, rows_of(j)], rsx.at[j - 1, zc], rsx_s.at[j - 1, zc], rsx_r.at[j - 1, zc], at_x(j)
        )

    def z_part(k):
        o = far_first(k)
        return remote(red.at[far(k)], rsz.at[o], rsz_s.at[o], rsz_r.at[o], at_z(o))

    def send_parts(k):
        for j in range(1, X):
            x_part(j, far(k)).start()

    def column_product(load_first, send):
        def chunk(k):
            zc = far(k)
            if load_first:
                load(k).wait()
                for t in range(0, 1024, 128):
                    high, low = split(stage[zc, t // 512, t % 512 : t % 512 + 128])
                    hhi[zc, t : t + 128] = high
                    hlo[zc, t : t + 128] = low
            both = dot(lhs[...], hhi[zc])
            part[zc] = both[: 2 * K] + both[2 * K :] + dot(lhs[: 2 * K], hlo[zc])
            if send:
                send_parts(k)

        loop(Z, chunk)

    def column_sum():
        def chunk(k):
            zc = far(k)
            total = part[zc, rows_of(0)]
            for j in range(1, X):
                x_part(j, zc).wait_recv()
                total = total + rsx[j - 1, zc]
            red[zc] = total

            @pl.when(k < Z - 1)
            def _():
                z_part(k).start()

        loop(Z, chunk)


    def z_whole(o, zc):
        block = gath.at[zc, rows_of(0)]
        return remote(block, block, agz_s.at[o], agz_r.at[o], at_z(o))

    def x_whole(j, zc, shift):
        block = gath.at[zc, rows_of(shift)]
        return remote(block, block, agx_s.at[j - 1, zc], agx_r.at[j - 1, zc], at_x(j))

    def column_gather(tiles):
        def last(k, total):
            z_part(k).wait_recv()
            return total + rsz[far_first(k)]

        gath[z, rows_of(0)] = lax.fori_loop(0, Z - 1, last, red[z])
        loop(Z - 1, lambda k: z_whole(far_first(k), z).start())
        for j in range(1, X):
            x_whole(j, z, 0).start()

        def forward(k):
            z_whole(near_first(k), near(k)).wait_recv()
            for j in range(1, X):
                x_whole(j, near(k), 0).start()

        def step(k, tiles):
            tiles = factor_block(k, tiles)
            forward(k + 1)
            return tiles

        if tiles is None:
            loop(Z - 1, lambda k: forward(k + 1))
            return None
        tiles = lax.fori_loop(0, K // 8, step, tiles)
        forward(Z - 1)
        return factor_end(tiles)

    def column_sent():
        def chunk(k):
            for j in range(1, X):
                x_part(j, k).wait_send()
                x_whole(j, k, 0).wait_send()

            @pl.when(k < Z - 1)
            def _():
                z_part(k).wait_send()
                z_whole(far_first(k), z).wait_send()

        loop(Z, chunk)

    def c_gram(t, k):
        return remote(gsrc, gyc.at[t, k], gyc_s.at[t, k], gyc_r.at[t, k], at_c(k))

    def c_scatter(t, k):
        return remote(scat.at[t, (c + k) & 7], ypc.at[t], sc_s.at[t, k], sc_r.at[t], at_c(k))

    def c_part(k):
        return remote(pk.at[(c + k) & 7], rsy.at[k], rsy_s.at[k], rsy_r.at[k], at_c(k))

    def row_product(t, factor):
        acc[...] = jnp.zeros_like(acc)
        acc2[...] = jnp.zeros_like(acc2)
        gsum[...] = jnp.zeros_like(gsum)

        def receive(k):
            zc = near(k)
            for j in range(1, X):
                x_whole(j, zc, X - j).wait_recv()
            block = gath[zc]
            if factor is not None:
                block = in_parts(dot, factor, block)
            ybuf[zc] = block
            high, low = split(block)
            acc[...] += dot_nt(jnp.concatenate([high, low], axis=0), hhi[zc])
            acc2[...] += dot_nt(high, hlo[zc])
            gsum[...] += gram_planes(block[:K], block[K:])

        loop(Z, receive)
        total = acc[: 2 * K] + acc[2 * K :] + acc2[...]
        re = total[:K, :512] - total[K:, 512:]
        im = total[K:, :512] + total[:K, 512:]
        for q in range(4):
            even, odd = pack_pair(re[:, 128 * q : 128 * q + 128], im[:, 128 * q : 128 * q + 128])
            pk[2 * q], pk[2 * q + 1] = even, odd
        for k in range(1, C):
            c_part(k).start()

        @pl.when(c == z)
        def _():
            for q in range(4):
                chunk = ybuf.at[2 * x + q // 2]
                part_lanes = slice((q % 2) * 128, (q % 2) * 128 + 128)
                even, odd = pack_pair(chunk[:K, part_lanes], chunk[K:, part_lanes])
                scat[t, 2 * q], scat[t, 2 * q + 1] = even, odd
            for k in range(1, C):
                c_scatter(t, k).start()
            ypc[t] = scat[t, c]

        gsrc[...] = pack_triangle(gsum[...])
        for k in range(1, C):
            c_gram(t, k).start()

    def row_sum():
        total = pk[c]
        for k in range(1, C):
            c_part(k).wait_recv()
            total = total + rsy[k]
        return total

    def c_factor(t):
        total = gsrc[...]
        for k in range(1, C):
            c_gram(t, k).wait_recv()
            total = total + gyc[t, k]
        return inverse_factor(unpack_triangle(total * (1.0 / N)))

    def scattered(t):
        @pl.when(c != z)
        def _():
            c_scatter(t, 1).wait_recv()

        return ypc[t]

    def row_sent(t):
        for k in range(1, C):
            c_part(k).wait_send()
            c_gram(t, k).wait_send()

        @pl.when(c == z)
        def _():
            for k in range(1, C):
                c_scatter(t, k).wait_send()

    v_re, v_im = initial[0], initial[1]
    set_left(v_re, v_im)
    pl.semaphore_wait(barrier, len(partners))
    column_product(True, True)
    for q in range(4):
        even, odd = pack_pair(v_re[:, 128 * q : 128 * q + 128], v_im[:, 128 * q : 128 * q + 128])
        pk[2 * q], pk[2 * q + 1] = even, odd
    v_piece = pk[c]
    column_sum()
    column_gather(None)
    row_product(0, None)
    z2_piece = row_sum()
    gy[c] = z2_piece

    def c_whole(k, src):
        return remote(gy.at[src], gy.at[src], agy_s.at[k], agy_r.at[k], at_c(k))

    for k in range(1, C):
        c_whole(k, c).start()
    inv1 = c_factor(0)
    column_sent()
    for k in range(1, C):
        c_whole(k, (c + C - k) & 7).wait_recv()
    pairs = [unpack_pair(gy[2 * q], gy[2 * q + 1]) for q in range(4)]
    block = jnp.concatenate(
        [jnp.concatenate([pair[p] for pair in pairs], axis=1) for p in range(2)], axis=0
    )
    block = in_parts(dot, embedded(inv1), block)
    set_left(block[:K], block[K:])
    gxs[...] = pack_triangle(gram_planes(block[:K], block[K:]))

    def x_gram(j):
        return remote(gxs, gx.at[j], gx_s.at[j], gx_r.at[j], at_x(j))

    def z_gram(o):
        return remote(gzs, gz.at[o], gz_s.at[o], gz_r.at[o], at_z(o))

    for j in range(1, X):
        x_gram(j).start()
    column_product(False, True)
    total = gxs[...]
    for j in range(1, X):
        x_gram(j).wait_recv()
        total = total + gx[j]
    gzs[...] = total
    for o in range(1, Z):
        z_gram(o).start()
    row_sent(0)
    y2_piece = apply_packed(inv1, z2_piece)
    y1_piece = scattered(0)
    psrc[:K] = gram_packed(v_piece, y1_piece)
    psrc[K : 2 * K] = conj_apply_packed(inv1, gram_packed(y1_piece, y2_piece))
    column_sum()
    total = gzs[...]
    for o in range(1, Z):
        z_gram(o).wait_recv()
        total = total + gz[o]
    inv2 = column_gather(factor_start(unpack_triangle(total * (1.0 / N))))
    row_product(1, embedded(inv2))
    z4_piece = row_sum()


    def g_c(m, k):
        return remote(g4.at[m, 0], g4y.at[m, k], g4y_s.at[m, k], g4y_r.at[m, k], at_c(k))

    def g_x(m, j):
        return remote(g4.at[m, 1], g4x.at[m, j], g4x_s.at[m, j], g4x_r.at[m, j], at_x(j))

    def g_z(m, o):
        return remote(g4.at[m, 2], g4z.at[m, o], g4z_s.at[m, o], g4z_r.at[m, o], at_z(o))

    def slab(shift):
        return pl.ds(pl.multiple_of(((c + shift) & 7) * RB, 8), RB)

    def p_c(k):
        return remote(psrc.at[slab(k)], py.at[k], py_s.at[k], py_r.at[k], at_c(k))

    def p_x(j):
        return remote(px.at[0], px.at[j], px_s.at[j], px_r.at[j], at_x(j))

    def p_z(o):
        return remote(pz.at[0], pz.at[o], pz_s.at[o], pz_r.at[o], at_z(o))

    def p_all(k, shift):
        return remote(pall.at[slab(shift)], pall.at[slab(shift)], pa_s.at[k], pa_r.at[k], at_c(k))

    def added(total, n, copy, slots):
        for i in range(1, n):
            copy(i).wait_recv()
            total = total + slots[i]
        return total

    def last_start(m, total):
        g4[m, 0] = total
        for k in range(1, C):
            g_c(m, k).start()
        return total

    def last_x(m, total):
        for k in range(1, C):
            g_c(m, k).wait_recv()
            total = total + g4y[m, k]
        g4[m, 1] = total
        for j in range(1, X):
            g_x(m, j).start()
        return total

    def last_z(m, total):
        for j in range(1, X):
            g_x(m, j).wait_recv()
            total = total + g4x[m, j]
        g4[m, 2] = total
        for o in range(1, Z):
            g_z(m, o).start()
        return total

    def last_end(m, total):
        for o in range(1, Z):
            g_z(m, o).wait_recv()
            total = total + g4z[m, o]
        return unpack_triangle(total * (1.0 / N))

    gram = last_start(0, pack_triangle(gram_packed(z4_piece, z4_piece)))
    y3_piece = scattered(1)
    projection = last_start(1, pack_triangle(gram_packed(y3_piece, z4_piece)))
    psrc[2 * K : 3 * K] = conj_apply_packed(inv2, gram_packed(y2_piece, y3_piece))
    psrc[3 * K :] = jnp.zeros((K, 128), F32)
    for k in range(1, C):
        p_c(k).start()
    inv3 = c_factor(1)
    gram = last_x(0, gram)
    y4_piece = apply_packed(inv3, z4_piece)
    projection = last_x(1, projection)
    gram = last_z(0, gram)
    px[0] = added(psrc[slab(0)], C, p_c, py)
    for j in range(1, X):
        p_x(j).start()
    projection = last_z(1, projection)
    pz[0] = added(px[0], X, p_x, px)
    for o in range(1, Z):
        p_z(o).start()
    column_sent()
    row_sent(1)
    for k in range(1, C):
        c_whole(k, c).wait_send()
        for m in range(2):
            g_c(m, k).wait_send()
        p_c(k).wait_send()
    for j in range(1, X):
        x_gram(j).wait_send()
        for m in range(2):
            g_x(m, j).wait_send()
        p_x(j).wait_send()
    for o in range(1, Z):
        z_gram(o).wait_send()
    gram = both_sides(inv3, last_end(0, gram))
    pall[slab(0)] = added(pz[0], Z, p_z, pz) * (1.0 / N)
    for k in range(1, C):
        p_all(k, 0).start()
    value = apply_packed(inverse_factor(gram), y4_piece)
    basis[0] = value[:, :64]
    basis[1] = pltpu.roll(value, 64, 1)[:, :64]
    for k in range(1, C):
        p_all(k, C - k).wait_recv()
    for t in range(ITERS):
        value = pall[K * t : K * t + K] if t < ITERS - 1 else both_sides(inv3, last_end(1, projection))
        ritz[t, 0] = value[:, :K]
        ritz[t, 1] = pltpu.roll(value, 64, 1)[:, :K]

    for k in range(1, C):
        p_all(k, 0).wait_send()
    for o in range(1, Z):
        for m in range(2):
            g_z(m, o).wait_send()
        p_z(o).wait_send()


def solution(mesh):
    dma = pltpu.SemaphoreType.DMA
    packed, piece = (K, 128), (RB, 128)
    scratch = [
        pltpu.VMEM((Z, 2, 512, CH), F32),
        pltpu.VMEM((Z, 1024, CH), BF16),
        pltpu.VMEM((Z, 1024, CH), BF16),
        pltpu.VMEM((4 * K, 1024), BF16),
        pltpu.VMEM((Z, 2 * K, CH), F32),
        pltpu.VMEM((3, Z, RB, CH), F32),
        pltpu.VMEM((Z, RB, CH), F32),
        pltpu.VMEM((Z, RB, CH), F32),
        pltpu.VMEM((Z, 2 * K, CH), F32),
        pltpu.VMEM((Z, 2 * K, CH), F32),
        pltpu.VMEM((4 * K, 1024), F32),
        pltpu.VMEM((2 * K, 1024), F32),
        pltpu.VMEM((C, *packed), F32),
        pltpu.VMEM((C, *packed), F32),
        pltpu.VMEM((C, *packed), F32),
        pltpu.VMEM((2, C, *packed), F32),
        pltpu.VMEM((2, *packed), F32),
        pltpu.VMEM(packed, F32),
        pltpu.VMEM(piece, F32),
        pltpu.VMEM((2, C, *piece), F32),
        pltpu.VMEM(piece, F32),
        pltpu.VMEM((X, *piece), F32),
        pltpu.VMEM(piece, F32),
        pltpu.VMEM((Z, *piece), F32),
        pltpu.VMEM((2, 3, *piece), F32),
        pltpu.VMEM((2, C, *piece), F32),
        pltpu.VMEM((2, X, *piece), F32),
        pltpu.VMEM((2, Z, *piece), F32),
        pltpu.VMEM((4 * K, 128), F32),
        pltpu.VMEM((C, *piece), F32),
        pltpu.VMEM((X, *piece), F32),
        pltpu.VMEM((Z, *piece), F32),
        pltpu.VMEM((4 * K, 128), F32),
        dma((Z,)),
        dma((3, Z)), dma((3, Z)), dma((Z,)), dma((Z,)),
        dma((Z,)), dma((Z,)), dma((3, Z)), dma((3, Z)),
        dma((C,)), dma((C,)), dma((C,)), dma((C,)),
        dma((2, C)), dma((2,)), dma((2, C)), dma((2, C)),
        dma((X,)), dma((X,)), dma((Z,)), dma((Z,)),
        dma((2, C)), dma((2, C)), dma((2, X)), dma((2, X)), dma((2, Z)), dma((2, Z)),
        dma((C,)), dma((C,)), dma((X,)), dma((X,)), dma((Z,)), dma((Z,)), dma((C,)), dma((C,)),
    ]
    vmem = pl.BlockSpec(memory_space=pltpu.VMEM)

    def body(coupling, initial):
        return pl.pallas_call(
            kernel,
            name="subspace",
            out_shape=(
                jax.ShapeDtypeStruct((2, K, 64), F32),
                jax.ShapeDtypeStruct((ITERS, 2, K, K), F32),
            ),
            in_specs=[pl.BlockSpec(memory_space=pl.ANY), vmem],
            out_specs=(vmem, vmem),
            scratch_shapes=scratch,
            compiler_params=pltpu.CompilerParams(
                collective_id=0, has_side_effects=True, vmem_limit_bytes=56 * 1024 * 1024
            ),
        )(coupling, initial)

    return jax.shard_map(
        body,
        mesh=mesh,
        in_specs=(P(None, "rows", "cols"), P(None, None, "rows")),
        out_specs=(P(None, None, ("rows", "cols")), P()),
        check_vma=False,
    )
```

```python
import jax
import jax.numpy as jnp
from jax import lax
from jax.experimental import pallas as pl
from jax.experimental.pallas import tpu as pltpu
from jax.sharding import PartitionSpec as P

N = 16384
K = 48
ITERS = 4
X, Z, C = 4, 8, 8
CH = 256
RB = 2 * K // X
F32, BF16 = jnp.float32, jnp.bfloat16
MESH = pl.DeviceIdType.MESH
NT = (((1,), (1,)), ((), ()))


def dot(a, b):
    return jnp.dot(a, b, preferred_element_type=F32)


def dot_nt(a, b):
    return lax.dot_general(a, b, NT, preferred_element_type=F32)


def split(value):
    high = value.astype(BF16)
    return high, (value - high.astype(F32)).astype(BF16)


def in_parts(product, a, b):
    (ah, al), (bh, bl) = split(a), split(b)
    return product(ah, bh) + (product(ah, bl) + product(al, bh))


def lanes(shape):
    return lax.broadcasted_iota(jnp.int32, shape, 1)


def turned(packed):
    rolled = pltpu.roll(packed, 64, 1)
    return jnp.where(lanes(packed.shape) < 64, rolled, -rolled)


def stacked_rows(first, second):
    gap = jnp.zeros((64 - K, first.shape[1]), first.dtype)
    return jnp.concatenate([first, gap, second, gap], axis=0)


def gram_packed(left, right):
    return in_parts(dot_nt, left, stacked_rows(right, turned(right)))


def gram_planes(re, im):
    return in_parts(dot_nt, re, stacked_rows(re, im)) + in_parts(dot_nt, im, stacked_rows(im, -re))


def planes_of(packed):
    low = lanes(packed.shape) < 64
    return jnp.where(low, packed, 0.0), jnp.where(low, pltpu.roll(packed, 64, 1), 0.0)


def apply_packed(matrix, packed):
    re, im = planes_of(matrix)
    return in_parts(dot, re[:, :K], packed) - in_parts(dot, im[:, :K], turned(packed))


def conj_apply_packed(matrix, packed):
    re, im = planes_of(matrix)
    return in_parts(dot, re[:, :K], packed) + in_parts(dot, im[:, :K], turned(packed))


def embedded(matrix):
    re, im = planes_of(matrix)
    upper = re - pltpu.roll(im, K, 1)
    lower = im + pltpu.roll(re, K, 1)
    return jnp.concatenate([upper, lower], axis=0)[:, : 2 * K]


def factor_start(gram):
    lane = lanes((K, 128))
    row = lax.broadcasted_iota(jnp.int32, (K, 128), 0)
    low = lane < 64
    re = jnp.where(low, gram, jnp.where(lane - 64 == row, 1.0, 0.0))
    im = jnp.where(low, pltpu.roll(gram, 64, 1), 0.0)
    return tuple(plane[t : t + 8] for plane in (re, im) for t in range(0, K, 8))


def factor_block(block, tiles):
    n = K // 8
    re, im = list(tiles[:n]), list(tiles[n:])
    below = lax.broadcasted_iota(jnp.int32, (8, 1), 0)
    open_tile = [None] + [jnp.where(block + t < n, 1.0, 0.0) for t in range(1, n)]
    for s in range(8):
        row_re, row_im = re[0][s : s + 1], im[0][s : s + 1]
        inv = 1.0 / row_re[:, s : s + 1]
        for t in range(n):
            if t == 0:
                m_re = jnp.where(below > s, re[t][:, s : s + 1] * inv, 0.0)
                m_im = jnp.where(below > s, im[t][:, s : s + 1] * inv, 0.0)
            else:
                m_re = re[t][:, s : s + 1] * (inv * open_tile[t])
                m_im = im[t][:, s : s + 1] * (inv * open_tile[t])
            re[t], im[t] = (
                re[t] - (m_re * row_re - m_im * row_im),
                im[t] - (m_re * row_im + m_im * row_re),
            )
    moved = [pltpu.roll(tile, 128 - 8, 1) for tile in re[1:] + re[:1] + im[1:] + im[:1]]
    return tuple(moved)


def factor_end(tiles):
    n = K // 8
    re = pltpu.roll(jnp.concatenate(tiles[:n], axis=0), K, 1)
    im = pltpu.roll(jnp.concatenate(tiles[n:], axis=0), K, 1)
    lane = lanes((K, 128))
    row = lax.broadcasted_iota(jnp.int32, (K, 128), 0)
    pivot = jnp.sum(jnp.where(lane == row, re, 0.0), axis=1, keepdims=True)
    scale = 1.0 / jnp.sqrt(pivot)
    return jnp.where(lane < 64, pltpu.roll(re, 64, 1), im) * scale


def inverse_factor(gram):
    return factor_end(lax.fori_loop(0, K // 8, factor_block, factor_start(gram)))


def both_sides(matrix, packed):
    left = conj_apply_packed(matrix, packed)
    low = lanes(matrix.shape) < 64
    return in_parts(dot_nt, left, stacked_rows(jnp.where(low, matrix, -matrix), pltpu.roll(matrix, 64, 1)))


def pack_pair(re, im):
    low = lanes(re.shape) < 64
    even = jnp.where(low, re, pltpu.roll(im, 64, 1))
    odd = jnp.where(low, pltpu.roll(re, 64, 1), im)
    return even, odd


def pack_triangle(packed):
    lane, row = lanes(packed.shape), lax.broadcasted_iota(jnp.int32, packed.shape, 0)
    one = jnp.where(lane >= row, packed, pltpu.roll(packed, 64, 1))
    return jnp.where(lane[:RB] < 64, one[:RB], pltpu.roll(one[RB:], 64, 1))


def unpack_triangle(half):
    low = lanes(half.shape) < 64
    upper = jnp.where(low, half, 0.0)
    lower = jnp.where(low, pltpu.roll(half, 64, 1), 0.0)
    tri = jnp.concatenate([upper, lower], axis=0)
    lane, row = lanes((K, 128)), lax.broadcasted_iota(jnp.int32, (K, 128), 0)
    other = jnp.concatenate([tri, jnp.zeros((128 - K, 128), F32)], axis=0).T[:K]
    re = jnp.where(lane >= row, tri, other)
    im = jnp.where(lane < row, tri, jnp.where(lane > row, -other, 0.0))
    return jnp.where(lane < 64, re, pltpu.roll(im, 64, 1))


def unpack_pair(even, odd):
    low = lanes(even.shape) < 64
    re = jnp.where(low, even, pltpu.roll(odd, 64, 1))
    im = jnp.where(low, pltpu.roll(even, 64, 1), odd)
    return re, im


def far_first(k):
    return 4 + (k >> 1) * (1 - (k & 1)) - ((k + 1) >> 1) * (k & 1)


def near_first(k):
    return far_first(7 - k) & 7


def kernel(coupling, initial, basis, ritz, *scratch):
    (
        stage, hhi, hlo, lhs, part, rsx, red, rsz, gath, ybuf, acc, acc2,
        pk, rsy, gy, scat, ypc, gsum, gsrc, gyc, gxs, gx, gzs, gz,
        g4, g4y, g4x, g4z, psrc, py, px, pz, pall,
        hsem, big, rw_s, rw_r, aw_s, aw_r, rsx_s, rsx_r, rsz_s, rsz_r, agz_s, agz_r, agx_s, agx_r,
        rsy_s, rsy_r, agy_s, agy_r, sc_s, sc_r, gyc_s, gyc_r, gx_s, gx_r, gz_s, gz_r,
        g4y_s, g4y_r, g4x_s, g4x_r, g4z_s, g4z_r, py_s, py_r, px_s, px_r, pz_s, pz_r, pa_s, pa_r,
    ) = scratch
    r, c = lax.axis_index("rows"), lax.axis_index("cols")
    z, x = r >> 2, r & 3

    def at_x(j):
        return (z * X + ((x + j) & 3), c)

    def at_z(o):
        return (((z + o) & 7) * X + x, c)

    def at_c(k):
        return (r, (c + k) & 7)

    def remote(src, dst, send, recv, dev):
        return pltpu.make_async_remote_copy(
            src_ref=src, dst_ref=dst, send_sem=send, recv_sem=recv,
            device_id=dev, device_id_type=MESH,
        )

    def loop(n, f):
        def step(i, carry):
            f(i)
            return carry

        lax.fori_loop(0, n, step, 0)

    def rows_of(j):
        return pl.ds(pl.multiple_of(((x + j) & 3) * RB, 8), RB)

    def far(k):
        return (z + far_first(k)) & 7

    def near(k):
        return (z + 8 - near_first(k)) & 7

    def load(k):
        columns = pl.ds(pl.multiple_of(far(k) * CH, CH), CH)
        return pltpu.make_async_copy(coupling.at[:, :, columns], stage.at[far(k)], hsem.at[far(k)])

    loop(Z, lambda k: load(k).start())

    barrier = pltpu.get_barrier_semaphore()
    partners = [at_x(j) for j in range(1, X)] + [at_z(o) for o in range(1, Z)]
    partners += [at_c(k) for k in range(1, C)]
    for dev in partners:
        pl.semaphore_signal(barrier, inc=1, device_id=dev, device_id_type=MESH)

    def set_left(re, im):
        top = jnp.concatenate([re, im], axis=1)
        bottom = jnp.concatenate([im, -re], axis=1)
        high, low = split(jnp.concatenate([top, bottom], axis=0))
        lhs[...] = jnp.concatenate([high, low], axis=0)


    def x_part(j, zc):
        return remote(
            part.at[zc, rows_of(j)], rsx.at[j - 1, zc], rsx_s.at[j - 1, zc], rsx_r.at[j - 1, zc], at_x(j)
        )

    def z_part(k):
        o = far_first(k)
        return remote(red.at[far(k)], rsz.at[o], rsz_s.at[o], rsz_r.at[o], at_z(o))

    def send_parts(k):
        for j in (1, 3, 2):
            x_part(j, far(k)).start()

    def whole_part():
        return remote(part.at[far(0)], big, rw_s.at[0], rw_r.at[0], at_z(4))

    def column_product(load_first, send):
        def chunk(k):
            zc = far(k)
            if load_first:
                load(k).wait()
                for t in range(0, 1024, 128):
                    high, low = split(stage[zc, t // 512, t % 512 : t % 512 + 128])
                    hhi[zc, t : t + 128] = high
                    hlo[zc, t : t + 128] = low
            both = dot(lhs[...], hhi[zc])
            part[zc] = both[: 2 * K] + both[2 * K :] + dot(lhs[: 2 * K], hlo[zc])
            if send:

                @pl.when(k == 0)
                def _():
                    whole_part().start()

                @pl.when((k > 0) & (k < Z - 1))
                def _():
                    send_parts(k)

        loop(Z, chunk)

    def column_sum():
        def chunk(i):
            k = i + 1
            zc = far(k)

            @pl.when(k == 5)
            def _():
                whole_part().wait_recv()
                part[z] = part[z] + big[...]
                send_parts(Z - 1)

            total = part[zc, rows_of(0)]
            for j in range(1, X):
                x_part(j, zc).wait_recv()
                total = total + rsx[j - 1, zc]
            red[zc] = total

            @pl.when(k < Z - 1)
            def _():
                z_part(k).start()

        loop(Z - 1, chunk)


    def z_whole(o, zc):
        block = gath.at[zc, rows_of(0)]
        return remote(block, block, agz_s.at[o], agz_r.at[o], at_z(o))

    def x_whole(j, zc, shift):
        block = gath.at[zc, rows_of(shift)]
        return remote(block, block, agx_s.at[j - 1, zc], agx_r.at[j - 1, zc], at_x(j))

    def whole_block(zc):
        return remote(gath.at[zc], gath.at[zc], aw_s.at[0], aw_r.at[0], at_z(4))

    def column_gather(tiles):
        def last(k, total):
            z_part(k).wait_recv()
            return total + rsz[far_first(k)]

        gath[z, rows_of(0)] = lax.fori_loop(1, Z - 1, last, red[z])
        loop(Z - 2, lambda k: z_whole(far_first(k + 1), z).start())
        for j in (1, 3, 2):
            x_whole(j, z, 0).start()

        def forward(k):
            z_whole(near_first(k), near(k)).wait_recv()
            for j in (1, 3, 2):
                x_whole(j, near(k), 0).start()

            @pl.when(k == 2)
            def _():
                for j in range(1, X):
                    x_whole(j, z, X - j).wait_recv()
                whole_block(z).start()

        def step(k, tiles):
            tiles = factor_block(k, tiles)
            forward(k + 1)
            return tiles

        if tiles is None:
            loop(Z - 2, lambda k: forward(k + 1))
            return None
        tiles = lax.fori_loop(0, K // 8, step, tiles)
        return factor_end(tiles)

    def column_sent():
        def chunk(i):
            k = i + 1
            for j in range(1, X):
                x_part(j, far(k)).wait_send()
                x_whole(j, far(k), 0).wait_send()

            @pl.when(k < Z - 1)
            def _():
                z_part(k).wait_send()
                z_whole(far_first(k), z).wait_send()

        loop(Z - 1, chunk)
        whole_part().wait_send()
        whole_block(z).wait_send()

    def c_gram(t, k):
        return remote(gsrc, gyc.at[t, k], gyc_s.at[t, k], gyc_r.at[t, k], at_c(k))

    def c_scatter(t, k):
        return remote(scat.at[t, (c + k) & 7], ypc.at[t], sc_s.at[t, k], sc_r.at[t], at_c(k))

    def c_part(k):
        return remote(pk.at[(c + k) & 7], rsy.at[k], rsy_s.at[k], rsy_r.at[k], at_c(k))

    def row_product(t, factor):
        acc[...] = jnp.zeros_like(acc)
        acc2[...] = jnp.zeros_like(acc2)
        gsum[...] = jnp.zeros_like(gsum)

        def receive(k):
            zc = near(k)

            @pl.when((k > 0) & (k < Z - 1))
            def _():
                for j in range(1, X):
                    x_whole(j, zc, X - j).wait_recv()

            @pl.when(k == Z - 1)
            def _():
                whole_block(zc).wait_recv()

            block = gath[zc]
            if factor is not None:
                block = in_parts(dot, factor, block)
            ybuf[zc] = block
            high, low = split(block)
            acc[...] += dot_nt(jnp.concatenate([high, low], axis=0), hhi[zc])
            acc2[...] += dot_nt(high, hlo[zc])
            gsum[...] += gram_planes(block[:K], block[K:])

        loop(Z, receive)
        total = acc[: 2 * K] + acc[2 * K :] + acc2[...]
        re = total[:K, :512] - total[K:, 512:]
        im = total[K:, :512] + total[:K, 512:]
        for q in range(4):
            even, odd = pack_pair(re[:, 128 * q : 128 * q + 128], im[:, 128 * q : 128 * q + 128])
            pk[2 * q], pk[2 * q + 1] = even, odd
        for k in range(1, C):
            c_part(k).start()

        @pl.when(c == z)
        def _():
            for q in range(4):
                chunk = ybuf.at[2 * x + q // 2]
                part_lanes = slice((q % 2) * 128, (q % 2) * 128 + 128)
                even, odd = pack_pair(chunk[:K, part_lanes], chunk[K:, part_lanes])
                scat[t, 2 * q], scat[t, 2 * q + 1] = even, odd
            for k in range(1, C):
                c_scatter(t, k).start()
            ypc[t] = scat[t, c]

        gsrc[...] = pack_triangle(gsum[...])
        for k in range(1, C):
            c_gram(t, k).start()

    def row_sum():
        total = pk[c]
        for k in range(1, C):
            c_part(k).wait_recv()
            total = total + rsy[k]
        return total

    def c_factor(t):
        total = gsrc[...]
        for k in range(1, C):
            c_gram(t, k).wait_recv()
            total = total + gyc[t, k]
        return inverse_factor(unpack_triangle(total * (1.0 / N)))

    def scattered(t):
        @pl.when(c != z)
        def _():
            c_scatter(t, 1).wait_recv()

        return ypc[t]

    def row_sent(t):
        for k in range(1, C):
            c_part(k).wait_send()
            c_gram(t, k).wait_send()

        @pl.when(c == z)
        def _():
            for k in range(1, C):
                c_scatter(t, k).wait_send()

    v_re, v_im = initial[0], initial[1]
    set_left(v_re, v_im)
    pl.semaphore_wait(barrier, len(partners))
    column_product(True, True)
    for q in range(4):
        even, odd = pack_pair(v_re[:, 128 * q : 128 * q + 128], v_im[:, 128 * q : 128 * q + 128])
        pk[2 * q], pk[2 * q + 1] = even, odd
    v_piece = pk[c]
    column_sum()
    column_gather(None)
    row_product(0, None)
    z2_piece = row_sum()
    gy[c] = z2_piece

    def c_whole(k, src):
        return remote(gy.at[src], gy.at[src], agy_s.at[k], agy_r.at[k], at_c(k))

    for k in range(1, C):
        c_whole(k, c).start()
    inv1 = c_factor(0)
    column_sent()
    for k in range(1, C):
        c_whole(k, (c + C - k) & 7).wait_recv()
    pairs = [unpack_pair(gy[2 * q], gy[2 * q + 1]) for q in range(4)]
    block = jnp.concatenate(
        [jnp.concatenate([pair[p] for pair in pairs], axis=1) for p in range(2)], axis=0
    )
    block = in_parts(dot, embedded(inv1), block)
    set_left(block[:K], block[K:])
    gxs[...] = pack_triangle(gram_planes(block[:K], block[K:]))

    def x_gram(j):
        return remote(gxs, gx.at[j], gx_s.at[j], gx_r.at[j], at_x(j))

    def z_gram(o):
        return remote(gzs, gz.at[o], gz_s.at[o], gz_r.at[o], at_z(o))

    for j in range(1, X):
        x_gram(j).start()
    column_product(False, True)
    total = gxs[...]
    for j in range(1, X):
        x_gram(j).wait_recv()
        total = total + gx[j]
    gzs[...] = total
    for o in range(1, Z):
        z_gram(o).start()
    row_sent(0)
    y2_piece = apply_packed(inv1, z2_piece)
    y1_piece = scattered(0)
    psrc[:K] = gram_packed(v_piece, y1_piece)
    psrc[K : 2 * K] = conj_apply_packed(inv1, gram_packed(y1_piece, y2_piece))
    column_sum()
    total = gzs[...]
    for o in range(1, Z):
        z_gram(o).wait_recv()
        total = total + gz[o]
    inv2 = column_gather(factor_start(unpack_triangle(total * (1.0 / N))))
    row_product(1, embedded(inv2))
    z4_piece = row_sum()


    def g_c(m, k):
        return remote(g4.at[m, 0], g4y.at[m, k], g4y_s.at[m, k], g4y_r.at[m, k], at_c(k))

    def g_x(m, j):
        return remote(g4.at[m, 1], g4x.at[m, j], g4x_s.at[m, j], g4x_r.at[m, j], at_x(j))

    def g_z(m, o):
        return remote(g4.at[m, 2], g4z.at[m, o], g4z_s.at[m, o], g4z_r.at[m, o], at_z(o))

    def slab(shift):
        return pl.ds(pl.multiple_of(((c + shift) & 7) * RB, 8), RB)

    def p_c(k):
        return remote(psrc.at[slab(k)], py.at[k], py_s.at[k], py_r.at[k], at_c(k))

    def p_x(j):
        return remote(px.at[0], px.at[j], px_s.at[j], px_r.at[j], at_x(j))

    def p_z(o):
        return remote(pz.at[0], pz.at[o], pz_s.at[o], pz_r.at[o], at_z(o))

    def p_all(k, shift):
        return remote(pall.at[slab(shift)], pall.at[slab(shift)], pa_s.at[k], pa_r.at[k], at_c(k))

    def added(total, n, copy, slots):
        for i in range(1, n):
            copy(i).wait_recv()
            total = total + slots[i]
        return total

    def last_start(m, total):
        g4[m, 0] = total
        for k in range(1, C):
            g_c(m, k).start()
        return total

    def last_x(m, total):
        for k in range(1, C):
            g_c(m, k).wait_recv()
            total = total + g4y[m, k]
        g4[m, 1] = total
        for j in range(1, X):
            g_x(m, j).start()
        return total

    def last_z(m, total):
        for j in range(1, X):
            g_x(m, j).wait_recv()
            total = total + g4x[m, j]
        g4[m, 2] = total
        for o in range(1, Z):
            g_z(m, o).start()
        return total

    def last_end(m, total):
        for o in range(1, Z):
            g_z(m, o).wait_recv()
            total = total + g4z[m, o]
        return unpack_triangle(total * (1.0 / N))

    gram = last_start(0, pack_triangle(gram_packed(z4_piece, z4_piece)))
    y3_piece = scattered(1)
    projection = last_start(1, pack_triangle(gram_packed(y3_piece, z4_piece)))
    psrc[2 * K : 3 * K] = conj_apply_packed(inv2, gram_packed(y2_piece, y3_piece))
    psrc[3 * K :] = jnp.zeros((K, 128), F32)
    for k in range(1, C):
        p_c(k).start()
    inv3 = c_factor(1)
    gram = last_x(0, gram)
    y4_piece = apply_packed(inv3, z4_piece)
    projection = last_x(1, projection)
    gram = last_z(0, gram)
    px[0] = added(psrc[slab(0)], C, p_c, py)
    for j in range(1, X):
        p_x(j).start()
    projection = last_z(1, projection)
    pz[0] = added(px[0], X, p_x, px)
    for o in range(1, Z):
        p_z(o).start()
    column_sent()
    row_sent(1)
    for k in range(1, C):
        c_whole(k, c).wait_send()
        for m in range(2):
            g_c(m, k).wait_send()
        p_c(k).wait_send()
    for j in range(1, X):
        x_gram(j).wait_send()
        for m in range(2):
            g_x(m, j).wait_send()
        p_x(j).wait_send()
    for o in range(1, Z):
        z_gram(o).wait_send()
    gram = both_sides(inv3, last_end(0, gram))
    pall[slab(0)] = added(pz[0], Z, p_z, pz) * (1.0 / N)
    for k in range(1, C):
        p_all(k, 0).start()
    value = apply_packed(inverse_factor(gram), y4_piece)
    basis[0] = value[:, :64]
    basis[1] = pltpu.roll(value, 64, 1)[:, :64]
    for k in range(1, C):
        p_all(k, C - k).wait_recv()
    for t in range(ITERS):
        value = pall[K * t : K * t + K] if t < ITERS - 1 else both_sides(inv3, last_end(1, projection))
        ritz[t, 0] = value[:, :K]
        ritz[t, 1] = pltpu.roll(value, 64, 1)[:, :K]

    for k in range(1, C):
        p_all(k, 0).wait_send()
    for o in range(1, Z):
        for m in range(2):
            g_z(m, o).wait_send()
        p_z(o).wait_send()


def solution(mesh):
    dma = pltpu.SemaphoreType.DMA
    packed, piece = (K, 128), (RB, 128)
    scratch = [
        pltpu.VMEM((Z, 2, 512, CH), F32),
        pltpu.VMEM((Z, 1024, CH), BF16),
        pltpu.VMEM((Z, 1024, CH), BF16),
        pltpu.VMEM((4 * K, 1024), BF16),
        pltpu.VMEM((Z, 2 * K, CH), F32),
        pltpu.VMEM((3, Z, RB, CH), F32),
        pltpu.VMEM((Z, RB, CH), F32),
        pltpu.VMEM((Z, RB, CH), F32),
        pltpu.VMEM((Z, 2 * K, CH), F32),
        pltpu.VMEM((Z, 2 * K, CH), F32),
        pltpu.VMEM((4 * K, 1024), F32),
        pltpu.VMEM((2 * K, 1024), F32),
        pltpu.VMEM((C, *packed), F32),
        pltpu.VMEM((C, *packed), F32),
        pltpu.VMEM((C, *packed), F32),
        pltpu.VMEM((2, C, *packed), F32),
        pltpu.VMEM((2, *packed), F32),
        pltpu.VMEM(packed, F32),
        pltpu.VMEM(piece, F32),
        pltpu.VMEM((2, C, *piece), F32),
        pltpu.VMEM(piece, F32),
        pltpu.VMEM((X, *piece), F32),
        pltpu.VMEM(piece, F32),
        pltpu.VMEM((Z, *piece), F32),
        pltpu.VMEM((2, 3, *piece), F32),
        pltpu.VMEM((2, C, *piece), F32),
        pltpu.VMEM((2, X, *piece), F32),
        pltpu.VMEM((2, Z, *piece), F32),
        pltpu.VMEM((4 * K, 128), F32),
        pltpu.VMEM((C, *piece), F32),
        pltpu.VMEM((X, *piece), F32),
        pltpu.VMEM((Z, *piece), F32),
        pltpu.VMEM((4 * K, 128), F32),
        dma((Z,)),
        pltpu.VMEM((2 * K, CH), F32),
        dma((1,)), dma((1,)), dma((1,)), dma((1,)),
        dma((3, Z)), dma((3, Z)), dma((Z,)), dma((Z,)),
        dma((Z,)), dma((Z,)), dma((3, Z)), dma((3, Z)),
        dma((C,)), dma((C,)), dma((C,)), dma((C,)),
        dma((2, C)), dma((2,)), dma((2, C)), dma((2, C)),
        dma((X,)), dma((X,)), dma((Z,)), dma((Z,)),
        dma((2, C)), dma((2, C)), dma((2, X)), dma((2, X)), dma((2, Z)), dma((2, Z)),
        dma((C,)), dma((C,)), dma((X,)), dma((X,)), dma((Z,)), dma((Z,)), dma((C,)), dma((C,)),
    ]
    vmem = pl.BlockSpec(memory_space=pltpu.VMEM)

    def body(coupling, initial):
        return pl.pallas_call(
            kernel,
            name="subspace",
            out_shape=(
                jax.ShapeDtypeStruct((2, K, 64), F32),
                jax.ShapeDtypeStruct((ITERS, 2, K, K), F32),
            ),
            in_specs=[pl.BlockSpec(memory_space=pl.ANY), vmem],
            out_specs=(vmem, vmem),
            scratch_shapes=scratch,
            compiler_params=pltpu.CompilerParams(
                collective_id=0, has_side_effects=True, vmem_limit_bytes=56 * 1024 * 1024
            ),
        )(coupling, initial)

    return jax.shard_map(
        body,
        mesh=mesh,
        in_specs=(P(None, "rows", "cols"), P(None, None, "rows")),
        out_specs=(P(None, None, ("rows", "cols")), P()),
        check_vma=False,
    )
```

```python
import jax
import jax.numpy as jnp
from jax import lax
from jax.experimental import pallas as pl
from jax.experimental.pallas import tpu as pltpu
from jax.sharding import PartitionSpec as P

N = 16384
K = 48
ITERS = 4
X, Z, C = 4, 8, 8
CH = 256
RB = 2 * K // X
F32, BF16 = jnp.float32, jnp.bfloat16
MESH = pl.DeviceIdType.MESH
NT = (((1,), (1,)), ((), ()))


def dot(a, b):
    return jnp.dot(a, b, preferred_element_type=F32)


def dot_nt(a, b):
    return lax.dot_general(a, b, NT, preferred_element_type=F32)


def split(value):
    high = value.astype(BF16)
    return high, (value - high.astype(F32)).astype(BF16)


def in_parts(product, a, b):
    (ah, al), (bh, bl) = split(a), split(b)
    return product(ah, bh) + (product(ah, bl) + product(al, bh))


def lanes(shape):
    return lax.broadcasted_iota(jnp.int32, shape, 1)


def turned(packed):
    rolled = pltpu.roll(packed, 64, 1)
    return jnp.where(lanes(packed.shape) < 64, rolled, -rolled)


def stacked_rows(first, second):
    gap = jnp.zeros((64 - K, first.shape[1]), first.dtype)
    return jnp.concatenate([first, gap, second, gap], axis=0)


def gram_packed(left, right):
    return in_parts(dot_nt, left, stacked_rows(right, turned(right)))


def gram_planes(re, im):
    return in_parts(dot_nt, re, stacked_rows(re, im)) + in_parts(dot_nt, im, stacked_rows(im, -re))


def planes_of(packed):
    low = lanes(packed.shape) < 64
    return jnp.where(low, packed, 0.0), jnp.where(low, pltpu.roll(packed, 64, 1), 0.0)


def apply_packed(matrix, packed):
    re, im = planes_of(matrix)
    return in_parts(dot, re[:, :K], packed) - in_parts(dot, im[:, :K], turned(packed))


def conj_apply_packed(matrix, packed):
    re, im = planes_of(matrix)
    return in_parts(dot, re[:, :K], packed) + in_parts(dot, im[:, :K], turned(packed))


def embedded(matrix):
    re, im = planes_of(matrix)
    upper = re - pltpu.roll(im, K, 1)
    lower = im + pltpu.roll(re, K, 1)
    return jnp.concatenate([upper, lower], axis=0)[:, : 2 * K]


def factor_start(gram):
    lane = lanes((K, 128))
    row = lax.broadcasted_iota(jnp.int32, (K, 128), 0)
    low = lane < 64
    re = jnp.where(low, gram, jnp.where(lane - 64 == row, 1.0, 0.0))
    im = jnp.where(low, pltpu.roll(gram, 64, 1), 0.0)
    return tuple(plane[t : t + 8] for plane in (re, im) for t in range(0, K, 8))


def factor_block(block, tiles):
    n = K // 8
    re, im = list(tiles[:n]), list(tiles[n:])
    below = lax.broadcasted_iota(jnp.int32, (8, 1), 0)
    open_tile = [None] + [jnp.where(block + t < n, 1.0, 0.0) for t in range(1, n)]
    for s in range(8):
        row_re, row_im = re[0][s : s + 1], im[0][s : s + 1]
        inv = 1.0 / row_re[:, s : s + 1]
        for t in range(n):
            if t == 0:
                m_re = jnp.where(below > s, re[t][:, s : s + 1] * inv, 0.0)
                m_im = jnp.where(below > s, im[t][:, s : s + 1] * inv, 0.0)
            else:
                m_re = re[t][:, s : s + 1] * (inv * open_tile[t])
                m_im = im[t][:, s : s + 1] * (inv * open_tile[t])
            re[t], im[t] = (
                re[t] - (m_re * row_re - m_im * row_im),
                im[t] - (m_re * row_im + m_im * row_re),
            )
    moved = [pltpu.roll(tile, 128 - 8, 1) for tile in re[1:] + re[:1] + im[1:] + im[:1]]
    return tuple(moved)


def factor_end(tiles):
    n = K // 8
    re = pltpu.roll(jnp.concatenate(tiles[:n], axis=0), K, 1)
    im = pltpu.roll(jnp.concatenate(tiles[n:], axis=0), K, 1)
    lane = lanes((K, 128))
    row = lax.broadcasted_iota(jnp.int32, (K, 128), 0)
    pivot = jnp.sum(jnp.where(lane == row, re, 0.0), axis=1, keepdims=True)
    scale = 1.0 / jnp.sqrt(pivot)
    return jnp.where(lane < 64, pltpu.roll(re, 64, 1), im) * scale


def inverse_factor(gram):
    return factor_end(lax.fori_loop(0, K // 8, factor_block, factor_start(gram)))


def both_sides(matrix, packed):
    left = conj_apply_packed(matrix, packed)
    low = lanes(matrix.shape) < 64
    return in_parts(dot_nt, left, stacked_rows(jnp.where(low, matrix, -matrix), pltpu.roll(matrix, 64, 1)))


def pack_pair(re, im):
    low = lanes(re.shape) < 64
    even = jnp.where(low, re, pltpu.roll(im, 64, 1))
    odd = jnp.where(low, pltpu.roll(re, 64, 1), im)
    return even, odd


def pack_triangle(packed):
    lane, row = lanes(packed.shape), lax.broadcasted_iota(jnp.int32, packed.shape, 0)
    one = jnp.where(lane >= row, packed, pltpu.roll(packed, 64, 1))
    return jnp.where(lane[:RB] < 64, one[:RB], pltpu.roll(one[RB:], 64, 1))


def unpack_triangle(half):
    low = lanes(half.shape) < 64
    upper = jnp.where(low, half, 0.0)
    lower = jnp.where(low, pltpu.roll(half, 64, 1), 0.0)
    tri = jnp.concatenate([upper, lower], axis=0)
    lane, row = lanes((K, 128)), lax.broadcasted_iota(jnp.int32, (K, 128), 0)
    other = jnp.concatenate([tri, jnp.zeros((128 - K, 128), F32)], axis=0).T[:K]
    re = jnp.where(lane >= row, tri, other)
    im = jnp.where(lane < row, tri, jnp.where(lane > row, -other, 0.0))
    return jnp.where(lane < 64, re, pltpu.roll(im, 64, 1))


def unpack_pair(even, odd):
    low = lanes(even.shape) < 64
    re = jnp.where(low, even, pltpu.roll(odd, 64, 1))
    im = jnp.where(low, pltpu.roll(even, 64, 1), odd)
    return re, im


def far_first(k):
    return 4 + (k >> 1) * (1 - (k & 1)) - ((k + 1) >> 1) * (k & 1)


def near_first(k):
    return far_first(7 - k) & 7


def results_kernel(value, projections, basis, ritz):
    basis[0] = value[:, :64]
    basis[1] = pltpu.roll(value[...], 64, 1)[:, :64]
    for t in range(ITERS):
        packed = projections[K * t : K * t + K]
        ritz[t, 0] = packed[:, :K]
        ritz[t, 1] = pltpu.roll(packed, 64, 1)[:, :K]


def kernel(coupling, initial, last_value, last_projections, *scratch):
    (
        stage, hhi, hlo, lhs, part, rsx, red, rsz, gath, ybuf, acc, acc2,
        pk, rsy, gy, scat, ypc, gsum, gsrc, gyc, gxs, gx, gzs, gz,
        g4, g4y, g4x, g4z, psrc, py, px, pz, pall,
        hsem, big, rw_s, rw_r, aw_s, aw_r, rsx_s, rsx_r, rsz_s, rsz_r, agz_s, agz_r, agx_s, agx_r,
        rsy_s, rsy_r, agy_s, agy_r, sc_s, sc_r, gyc_s, gyc_r, gx_s, gx_r, gz_s, gz_r,
        g4y_s, g4y_r, g4x_s, g4x_r, g4z_s, g4z_r, py_s, py_r, px_s, px_r, pz_s, pz_r, pa_s, pa_r,
    ) = scratch
    r, c = lax.axis_index("rows"), lax.axis_index("cols")
    z, x = r >> 2, r & 3

    def at_x(j):
        return (z * X + ((x + j) & 3), c)

    def at_z(o):
        return (((z + o) & 7) * X + x, c)

    def at_c(k):
        return (r, (c + k) & 7)

    def remote(src, dst, send, recv, dev):
        return pltpu.make_async_remote_copy(
            src_ref=src, dst_ref=dst, send_sem=send, recv_sem=recv,
            device_id=dev, device_id_type=MESH,
        )

    def loop(n, f):
        def step(i, carry):
            f(i)
            return carry

        lax.fori_loop(0, n, step, 0)

    def rows_of(j):
        return pl.ds(pl.multiple_of(((x + j) & 3) * RB, 8), RB)

    def far(k):
        return (z + far_first(k)) & 7

    def near(k):
        return (z + 8 - near_first(k)) & 7

    def load(k):
        columns = pl.ds(pl.multiple_of(far(k) * CH, CH), CH)
        return pltpu.make_async_copy(coupling.at[:, :, columns], stage.at[far(k)], hsem.at[far(k)])

    loop(Z, lambda k: load(k).start())

    barrier = pltpu.get_barrier_semaphore()
    partners = [at_x(j) for j in range(1, X)] + [at_z(o) for o in range(1, Z)]
    partners += [at_c(k) for k in range(1, C)]
    for dev in partners:
        pl.semaphore_signal(barrier, inc=1, device_id=dev, device_id_type=MESH)

    def set_left(re, im):
        top = jnp.concatenate([re, im], axis=1)
        bottom = jnp.concatenate([im, -re], axis=1)
        high, low = split(jnp.concatenate([top, bottom], axis=0))
        lhs[...] = jnp.concatenate([high, low], axis=0)


    def x_part(j, zc):
        return remote(
            part.at[zc, rows_of(j)], rsx.at[j - 1, zc], rsx_s.at[j - 1, zc], rsx_r.at[j - 1, zc], at_x(j)
        )

    def z_part(k):
        o = far_first(k)
        return remote(red.at[far(k)], rsz.at[o], rsz_s.at[o], rsz_r.at[o], at_z(o))

    def send_parts(k):
        for j in (1, 3, 2):
            x_part(j, far(k)).start()

    def whole_part():
        return remote(part.at[far(0)], big, rw_s.at[0], rw_r.at[0], at_z(4))

    def column_product(load_first, send):
        def chunk(k):
            zc = far(k)
            if load_first:
                load(k).wait()
                for t in range(0, 1024, 128):
                    high, low = split(stage[zc, t // 512, t % 512 : t % 512 + 128])
                    hhi[zc, t : t + 128] = high
                    hlo[zc, t : t + 128] = low
            both = dot(lhs[...], hhi[zc])
            part[zc] = both[: 2 * K] + both[2 * K :] + dot(lhs[: 2 * K], hlo[zc])
            if send:

                @pl.when(k == 0)
                def _():
                    whole_part().start()

                @pl.when((k > 0) & (k < Z - 1))
                def _():
                    send_parts(k)

        loop(Z, chunk)

    def column_sum():
        def chunk(i):
            k = i + 1
            zc = far(k)

            @pl.when(k == 5)
            def _():
                whole_part().wait_recv()
                part[z] = part[z] + big[...]
                send_parts(Z - 1)

            total = part[zc, rows_of(0)]
            for j in range(1, X):
                x_part(j, zc).wait_recv()
                total = total + rsx[j - 1, zc]
            red[zc] = total

            @pl.when(k < Z - 1)
            def _():
                z_part(k).start()

        loop(Z - 1, chunk)


    def z_whole(o, zc):
        block = gath.at[zc, rows_of(0)]
        return remote(block, block, agz_s.at[o], agz_r.at[o], at_z(o))

    def x_whole(j, zc, shift):
        block = gath.at[zc, rows_of(shift)]
        return remote(block, block, agx_s.at[j - 1, zc], agx_r.at[j - 1, zc], at_x(j))

    def whole_block(zc):
        return remote(gath.at[zc], gath.at[zc], aw_s.at[0], aw_r.at[0], at_z(4))

    def column_gather(tiles):
        def last(k, total):
            z_part(k).wait_recv()
            return total + rsz[far_first(k)]

        gath[z, rows_of(0)] = lax.fori_loop(1, Z - 1, last, red[z])
        loop(Z - 2, lambda k: z_whole(far_first(k + 1), z).start())
        for j in (1, 3, 2):
            x_whole(j, z, 0).start()

        def forward(k):
            z_whole(near_first(k), near(k)).wait_recv()
            for j in (1, 3, 2):
                x_whole(j, near(k), 0).start()

            @pl.when(k == 2)
            def _():
                for j in range(1, X):
                    x_whole(j, z, X - j).wait_recv()
                whole_block(z).start()

        def step(k, tiles):
            tiles = factor_block(k, tiles)
            forward(k + 1)
            return tiles

        if tiles is None:
            loop(Z - 2, lambda k: forward(k + 1))
            return None
        tiles = lax.fori_loop(0, K // 8, step, tiles)
        return factor_end(tiles)

    def column_sent():
        def chunk(i):
            k = i + 1
            for j in range(1, X):
                x_part(j, far(k)).wait_send()
                x_whole(j, far(k), 0).wait_send()

            @pl.when(k < Z - 1)
            def _():
                z_part(k).wait_send()
                z_whole(far_first(k), z).wait_send()

        loop(Z - 1, chunk)
        whole_part().wait_send()
        whole_block(z).wait_send()

    def c_gram(t, k):
        return remote(gsrc, gyc.at[t, k], gyc_s.at[t, k], gyc_r.at[t, k], at_c(k))

    def c_scatter(t, k):
        return remote(scat.at[t, (c + k) & 7], ypc.at[t], sc_s.at[t, k], sc_r.at[t], at_c(k))

    def c_part(k):
        return remote(pk.at[(c + k) & 7], rsy.at[k], rsy_s.at[k], rsy_r.at[k], at_c(k))

    def row_product(t, factor):
        acc[...] = jnp.zeros_like(acc)
        acc2[...] = jnp.zeros_like(acc2)
        gsum[...] = jnp.zeros_like(gsum)

        def receive(k):
            zc = near(k)

            @pl.when((k > 0) & (k < Z - 1))
            def _():
                for j in range(1, X):
                    x_whole(j, zc, X - j).wait_recv()

            @pl.when(k == Z - 1)
            def _():
                whole_block(zc).wait_recv()

            block = gath[zc]
            if factor is not None:
                block = in_parts(dot, factor, block)
            ybuf[zc] = block
            high, low = split(block)
            acc[...] += dot_nt(jnp.concatenate([high, low], axis=0), hhi[zc])
            acc2[...] += dot_nt(high, hlo[zc])
            gsum[...] += gram_planes(block[:K], block[K:])

        loop(Z, receive)
        total = acc[: 2 * K] + acc[2 * K :] + acc2[...]
        re = total[:K, :512] - total[K:, 512:]
        im = total[K:, :512] + total[:K, 512:]
        for q in range(4):
            even, odd = pack_pair(re[:, 128 * q : 128 * q + 128], im[:, 128 * q : 128 * q + 128])
            pk[2 * q], pk[2 * q + 1] = even, odd
        for k in range(1, C):
            c_part(k).start()

        @pl.when(c == z)
        def _():
            for q in range(4):
                chunk = ybuf.at[2 * x + q // 2]
                part_lanes = slice((q % 2) * 128, (q % 2) * 128 + 128)
                even, odd = pack_pair(chunk[:K, part_lanes], chunk[K:, part_lanes])
                scat[t, 2 * q], scat[t, 2 * q + 1] = even, odd
            for k in range(1, C):
                c_scatter(t, k).start()
            ypc[t] = scat[t, c]

        gsrc[...] = pack_triangle(gsum[...])
        for k in range(1, C):
            c_gram(t, k).start()

    def row_sum():
        total = pk[c]
        for k in range(1, C):
            c_part(k).wait_recv()
            total = total + rsy[k]
        return total

    def c_factor(t):
        total = gsrc[...]
        for k in range(1, C):
            c_gram(t, k).wait_recv()
            total = total + gyc[t, k]
        return inverse_factor(unpack_triangle(total * (1.0 / N)))

    def scattered(t):
        @pl.when(c != z)
        def _():
            c_scatter(t, 1).wait_recv()

        return ypc[t]

    def row_sent(t):
        for k in range(1, C):
            c_part(k).wait_send()
            c_gram(t, k).wait_send()

        @pl.when(c == z)
        def _():
            for k in range(1, C):
                c_scatter(t, k).wait_send()

    v_re, v_im = initial[0], initial[1]
    set_left(v_re, v_im)
    pl.semaphore_wait(barrier, len(partners))
    column_product(True, True)
    for q in range(4):
        even, odd = pack_pair(v_re[:, 128 * q : 128 * q + 128], v_im[:, 128 * q : 128 * q + 128])
        pk[2 * q], pk[2 * q + 1] = even, odd
    v_piece = pk[c]
    column_sum()
    column_gather(None)
    row_product(0, None)
    z2_piece = row_sum()
    gy[c] = z2_piece

    def c_whole(k, src):
        return remote(gy.at[src], gy.at[src], agy_s.at[k], agy_r.at[k], at_c(k))

    for k in range(1, C):
        c_whole(k, c).start()
    inv1 = c_factor(0)
    column_sent()
    for k in range(1, C):
        c_whole(k, (c + C - k) & 7).wait_recv()
    pairs = [unpack_pair(gy[2 * q], gy[2 * q + 1]) for q in range(4)]
    block = jnp.concatenate(
        [jnp.concatenate([pair[p] for pair in pairs], axis=1) for p in range(2)], axis=0
    )
    block = in_parts(dot, embedded(inv1), block)
    set_left(block[:K], block[K:])
    gxs[...] = pack_triangle(gram_planes(block[:K], block[K:]))

    def x_gram(j):
        return remote(gxs, gx.at[j], gx_s.at[j], gx_r.at[j], at_x(j))

    def z_gram(o):
        return remote(gzs, gz.at[o], gz_s.at[o], gz_r.at[o], at_z(o))

    for j in range(1, X):
        x_gram(j).start()
    column_product(False, True)
    total = gxs[...]
    for j in range(1, X):
        x_gram(j).wait_recv()
        total = total + gx[j]
    gzs[...] = total
    for o in range(1, Z):
        z_gram(o).start()
    row_sent(0)
    y2_piece = apply_packed(inv1, z2_piece)
    y1_piece = scattered(0)
    psrc[:K] = gram_packed(v_piece, y1_piece)
    psrc[K : 2 * K] = conj_apply_packed(inv1, gram_packed(y1_piece, y2_piece))
    column_sum()
    total = gzs[...]
    for o in range(1, Z):
        z_gram(o).wait_recv()
        total = total + gz[o]
    inv2 = column_gather(factor_start(unpack_triangle(total * (1.0 / N))))
    row_product(1, embedded(inv2))
    z4_piece = row_sum()


    def g_c(m, k):
        return remote(g4.at[m, 0], g4y.at[m, k], g4y_s.at[m, k], g4y_r.at[m, k], at_c(k))

    def g_x(m, j):
        return remote(g4.at[m, 1], g4x.at[m, j], g4x_s.at[m, j], g4x_r.at[m, j], at_x(j))

    def g_z(m, o):
        return remote(g4.at[m, 2], g4z.at[m, o], g4z_s.at[m, o], g4z_r.at[m, o], at_z(o))

    def slab(shift):
        return pl.ds(pl.multiple_of(((c + shift) & 7) * RB, 8), RB)

    def p_c(k):
        return remote(psrc.at[slab(k)], py.at[k], py_s.at[k], py_r.at[k], at_c(k))

    def p_x(j):
        return remote(px.at[0], px.at[j], px_s.at[j], px_r.at[j], at_x(j))

    def p_z(o):
        return remote(pz.at[0], pz.at[o], pz_s.at[o], pz_r.at[o], at_z(o))

    def p_all(k, shift):
        return remote(pall.at[slab(shift)], pall.at[slab(shift)], pa_s.at[k], pa_r.at[k], at_c(k))

    def added(total, n, copy, slots):
        for i in range(1, n):
            copy(i).wait_recv()
            total = total + slots[i]
        return total

    def last_start(m, total):
        g4[m, 0] = total
        for k in range(1, C):
            g_c(m, k).start()
        return total

    def last_x(m, total):
        for k in range(1, C):
            g_c(m, k).wait_recv()
            total = total + g4y[m, k]
        g4[m, 1] = total
        for j in range(1, X):
            g_x(m, j).start()
        return total

    def last_z(m, total):
        for j in range(1, X):
            g_x(m, j).wait_recv()
            total = total + g4x[m, j]
        g4[m, 2] = total
        for o in range(1, Z):
            g_z(m, o).start()
        return total

    def last_end(m, total):
        for o in range(1, Z):
            g_z(m, o).wait_recv()
            total = total + g4z[m, o]
        return unpack_triangle(total * (1.0 / N))

    gram = last_start(0, pack_triangle(gram_packed(z4_piece, z4_piece)))
    y3_piece = scattered(1)
    projection = last_start(1, pack_triangle(gram_packed(y3_piece, z4_piece)))
    psrc[2 * K : 3 * K] = conj_apply_packed(inv2, gram_packed(y2_piece, y3_piece))
    psrc[3 * K :] = jnp.zeros((K, 128), F32)
    for k in range(1, C):
        p_c(k).start()
    inv3 = c_factor(1)
    gram = last_x(0, gram)
    y4_piece = apply_packed(inv3, z4_piece)
    projection = last_x(1, projection)
    gram = last_z(0, gram)
    px[0] = added(psrc[slab(0)], C, p_c, py)
    for j in range(1, X):
        p_x(j).start()
    projection = last_z(1, projection)
    pz[0] = added(px[0], X, p_x, px)
    for o in range(1, Z):
        p_z(o).start()
    column_sent()
    row_sent(1)
    for k in range(1, C):
        c_whole(k, c).wait_send()
        for m in range(2):
            g_c(m, k).wait_send()
        p_c(k).wait_send()
    for j in range(1, X):
        x_gram(j).wait_send()
        for m in range(2):
            g_x(m, j).wait_send()
        p_x(j).wait_send()
    for o in range(1, Z):
        z_gram(o).wait_send()
    gram = both_sides(inv3, last_end(0, gram))
    pall[slab(0)] = added(pz[0], Z, p_z, pz) * (1.0 / N)
    for k in range(1, C):
        p_all(k, 0).start()
    last_value[...] = apply_packed(inverse_factor(gram), y4_piece)
    last_projections[3 * K :] = both_sides(inv3, last_end(1, projection))
    for k in range(1, C):
        p_all(k, C - k).wait_recv()
    last_projections[: 3 * K] = pall[: 3 * K]

    for k in range(1, C):
        p_all(k, 0).wait_send()
    for o in range(1, Z):
        for m in range(2):
            g_z(m, o).wait_send()
        p_z(o).wait_send()


def solution(mesh):
    dma = pltpu.SemaphoreType.DMA
    packed, piece = (K, 128), (RB, 128)
    scratch = [
        pltpu.VMEM((Z, 2, 512, CH), F32),
        pltpu.VMEM((Z, 1024, CH), BF16),
        pltpu.VMEM((Z, 1024, CH), BF16),
        pltpu.VMEM((4 * K, 1024), BF16),
        pltpu.VMEM((Z, 2 * K, CH), F32),
        pltpu.VMEM((3, Z, RB, CH), F32),
        pltpu.VMEM((Z, RB, CH), F32),
        pltpu.VMEM((Z, RB, CH), F32),
        pltpu.VMEM((Z, 2 * K, CH), F32),
        pltpu.VMEM((Z, 2 * K, CH), F32),
        pltpu.VMEM((4 * K, 1024), F32),
        pltpu.VMEM((2 * K, 1024), F32),
        pltpu.VMEM((C, *packed), F32),
        pltpu.VMEM((C, *packed), F32),
        pltpu.VMEM((C, *packed), F32),
        pltpu.VMEM((2, C, *packed), F32),
        pltpu.VMEM((2, *packed), F32),
        pltpu.VMEM(packed, F32),
        pltpu.VMEM(piece, F32),
        pltpu.VMEM((2, C, *piece), F32),
        pltpu.VMEM(piece, F32),
        pltpu.VMEM((X, *piece), F32),
        pltpu.VMEM(piece, F32),
        pltpu.VMEM((Z, *piece), F32),
        pltpu.VMEM((2, 3, *piece), F32),
        pltpu.VMEM((2, C, *piece), F32),
        pltpu.VMEM((2, X, *piece), F32),
        pltpu.VMEM((2, Z, *piece), F32),
        pltpu.VMEM((4 * K, 128), F32),
        pltpu.VMEM((C, *piece), F32),
        pltpu.VMEM((X, *piece), F32),
        pltpu.VMEM((Z, *piece), F32),
        pltpu.VMEM((4 * K, 128), F32),
        dma((Z,)),
        pltpu.VMEM((2 * K, CH), F32),
        dma((1,)), dma((1,)), dma((1,)), dma((1,)),
        dma((3, Z)), dma((3, Z)), dma((Z,)), dma((Z,)),
        dma((Z,)), dma((Z,)), dma((3, Z)), dma((3, Z)),
        dma((C,)), dma((C,)), dma((C,)), dma((C,)),
        dma((2, C)), dma((2,)), dma((2, C)), dma((2, C)),
        dma((X,)), dma((X,)), dma((Z,)), dma((Z,)),
        dma((2, C)), dma((2, C)), dma((2, X)), dma((2, X)), dma((2, Z)), dma((2, Z)),
        dma((C,)), dma((C,)), dma((X,)), dma((X,)), dma((Z,)), dma((Z,)), dma((C,)), dma((C,)),
    ]
    vmem = pl.BlockSpec(memory_space=pltpu.VMEM)

    def body(coupling, initial):
        value, projections = pl.pallas_call(
            kernel,
            name="subspace",
            out_shape=(
                jax.ShapeDtypeStruct((K, 128), F32),
                jax.ShapeDtypeStruct((ITERS * K, 128), F32),
            ),
            in_specs=[pl.BlockSpec(memory_space=pl.ANY), vmem],
            out_specs=(vmem, vmem),
            scratch_shapes=scratch,
            compiler_params=pltpu.CompilerParams(
                collective_id=0, has_side_effects=True, vmem_limit_bytes=56 * 1024 * 1024
            ),
        )(coupling, initial)
        return pl.pallas_call(
            results_kernel,
            name="results",
            out_shape=(
                jax.ShapeDtypeStruct((2, K, 64), F32),
                jax.ShapeDtypeStruct((ITERS, 2, K, K), F32),
            ),
            in_specs=[vmem, vmem],
            out_specs=(vmem, vmem),
        )(value, projections)

    return jax.shard_map(
        body,
        mesh=mesh,
        in_specs=(P(None, "rows", "cols"), P(None, None, "rows")),
        out_specs=(P(None, None, ("rows", "cols")), P()),
        check_vma=False,
    )
```

```python
import jax
import jax.numpy as jnp
from jax import lax
from jax.experimental import pallas as pl
from jax.experimental.pallas import tpu as pltpu
from jax.sharding import PartitionSpec as P

N = 16384
K = 48
ITERS = 4
X, Z, C = 4, 8, 8
CH = 256
RB = 2 * K // X
F32, BF16 = jnp.float32, jnp.bfloat16
MESH = pl.DeviceIdType.MESH
NT = (((1,), (1,)), ((), ()))


def dot(a, b):
    return jnp.dot(a, b, preferred_element_type=F32)


def dot_nt(a, b):
    return lax.dot_general(a, b, NT, preferred_element_type=F32)


def split(value):
    high = value.astype(BF16)
    return high, (value - high.astype(F32)).astype(BF16)


def in_parts(product, a, b):
    (ah, al), (bh, bl) = split(a), split(b)
    return product(ah, bh) + (product(ah, bl) + product(al, bh))


def lanes(shape):
    return lax.broadcasted_iota(jnp.int32, shape, 1)


def turned(packed):
    rolled = pltpu.roll(packed, 64, 1)
    return jnp.where(lanes(packed.shape) < 64, rolled, -rolled)


def stacked_rows(first, second):
    gap = jnp.zeros((64 - K, first.shape[1]), first.dtype)
    return jnp.concatenate([first, gap, second, gap], axis=0)


def gram_packed(left, right):
    return in_parts(dot_nt, left, stacked_rows(right, turned(right)))


def gram_planes(re, im):
    return in_parts(dot_nt, re, stacked_rows(re, im)) + in_parts(dot_nt, im, stacked_rows(im, -re))


def planes_of(packed):
    low = lanes(packed.shape) < 64
    return jnp.where(low, packed, 0.0), jnp.where(low, pltpu.roll(packed, 64, 1), 0.0)


def apply_packed(matrix, packed):
    re, im = planes_of(matrix)
    return in_parts(dot, re[:, :K], packed) - in_parts(dot, im[:, :K], turned(packed))


def conj_apply_packed(matrix, packed):
    re, im = planes_of(matrix)
    return in_parts(dot, re[:, :K], packed) + in_parts(dot, im[:, :K], turned(packed))


def embedded(matrix):
    re, im = planes_of(matrix)
    upper = re - pltpu.roll(im, K, 1)
    lower = im + pltpu.roll(re, K, 1)
    return jnp.concatenate([upper, lower], axis=0)[:, : 2 * K]


def factor_start(gram):
    lane = lanes((K, 128))
    row = lax.broadcasted_iota(jnp.int32, (K, 128), 0)
    low = lane < 64
    re = jnp.where(low, gram, jnp.where(lane - 64 == row, 1.0, 0.0))
    im = jnp.where(low, pltpu.roll(gram, 64, 1), 0.0)
    return tuple(plane[t : t + 8] for plane in (re, im) for t in range(0, K, 8))


def factor_block(block, tiles):
    n = K // 8
    re, im = list(tiles[:n]), list(tiles[n:])
    below = lax.broadcasted_iota(jnp.int32, (8, 1), 0)
    open_tile = [None] + [jnp.where(block + t < n, 1.0, 0.0) for t in range(1, n)]
    for s in range(8):
        row_re, row_im = re[0][s : s + 1], im[0][s : s + 1]
        inv = 1.0 / row_re[:, s : s + 1]
        for t in range(n):
            if t == 0:
                m_re = jnp.where(below > s, re[t][:, s : s + 1] * inv, 0.0)
                m_im = jnp.where(below > s, im[t][:, s : s + 1] * inv, 0.0)
            else:
                m_re = re[t][:, s : s + 1] * (inv * open_tile[t])
                m_im = im[t][:, s : s + 1] * (inv * open_tile[t])
            re[t], im[t] = (
                re[t] - (m_re * row_re - m_im * row_im),
                im[t] - (m_re * row_im + m_im * row_re),
            )
    moved = [pltpu.roll(tile, 128 - 8, 1) for tile in re[1:] + re[:1] + im[1:] + im[:1]]
    return tuple(moved)


def factor_end(tiles):
    n = K // 8
    re = pltpu.roll(jnp.concatenate(tiles[:n], axis=0), K, 1)
    im = pltpu.roll(jnp.concatenate(tiles[n:], axis=0), K, 1)
    lane = lanes((K, 128))
    row = lax.broadcasted_iota(jnp.int32, (K, 128), 0)
    pivot = jnp.sum(jnp.where(lane == row, re, 0.0), axis=1, keepdims=True)
    scale = 1.0 / jnp.sqrt(pivot)
    return jnp.where(lane < 64, pltpu.roll(re, 64, 1), im) * scale


def inverse_factor(gram):
    return factor_end(lax.fori_loop(0, K // 8, factor_block, factor_start(gram)))


def both_sides(matrix, packed):
    left = conj_apply_packed(matrix, packed)
    low = lanes(matrix.shape) < 64
    return in_parts(dot_nt, left, stacked_rows(jnp.where(low, matrix, -matrix), pltpu.roll(matrix, 64, 1)))


def pack_pair(re, im):
    low = lanes(re.shape) < 64
    even = jnp.where(low, re, pltpu.roll(im, 64, 1))
    odd = jnp.where(low, pltpu.roll(re, 64, 1), im)
    return even, odd


def pack_triangle(packed):
    lane, row = lanes(packed.shape), lax.broadcasted_iota(jnp.int32, packed.shape, 0)
    one = jnp.where(lane >= row, packed, pltpu.roll(packed, 64, 1))
    return jnp.where(lane[:RB] < 64, one[:RB], pltpu.roll(one[RB:], 64, 1))


def unpack_triangle(half):
    low = lanes(half.shape) < 64
    upper = jnp.where(low, half, 0.0)
    lower = jnp.where(low, pltpu.roll(half, 64, 1), 0.0)
    tri = jnp.concatenate([upper, lower], axis=0)
    lane, row = lanes((K, 128)), lax.broadcasted_iota(jnp.int32, (K, 128), 0)
    other = jnp.concatenate([tri, jnp.zeros((128 - K, 128), F32)], axis=0).T[:K]
    re = jnp.where(lane >= row, tri, other)
    im = jnp.where(lane < row, tri, jnp.where(lane > row, -other, 0.0))
    return jnp.where(lane < 64, re, pltpu.roll(im, 64, 1))


def unpack_pair(even, odd):
    low = lanes(even.shape) < 64
    re = jnp.where(low, even, pltpu.roll(odd, 64, 1))
    im = jnp.where(low, pltpu.roll(even, 64, 1), odd)
    return re, im


def far_first(k):
    return 4 + (k >> 1) * (1 - (k & 1)) - ((k + 1) >> 1) * (k & 1)


def near_first(k):
    return far_first(7 - k) & 7


def results_kernel(value, projections, basis, ritz):
    basis[0] = value[:, :64]
    basis[1] = pltpu.roll(value[...], 64, 1)[:, :64]
    for t in range(ITERS):
        packed = projections[K * t : K * t + K]
        ritz[t, 0] = packed[:, :K]
        ritz[t, 1] = pltpu.roll(packed, 64, 1)[:, :K]


def kernel(coupling, initial, last_value, last_projections, *scratch):
    (
        stage, hhi, hlo, lhs, part, rsx, red, rsz, gath, ybuf, acc, acc2,
        pk, rsy, gy, scat, ypc, gsum, gsrc, gyc, gxs, gx, gzs, gz,
        g4, g4y, g4x, g4z, psrc, py, px, pz, pall,
        hsem, big, rw_s, rw_r, aw_s, aw_r, rsx_s, rsx_r, rsz_s, rsz_r, agz_s, agz_r, agx_s, agx_r,
        rsy_s, rsy_r, agy_s, agy_r, sc_s, sc_r, gyc_s, gyc_r, gx_s, gx_r, gz_s, gz_r,
        g4y_s, g4y_r, g4x_s, g4x_r, g4z_s, g4z_r, py_s, py_r, px_s, px_r, pz_s, pz_r, pa_s, pa_r,
    ) = scratch
    r, c = lax.axis_index("rows"), lax.axis_index("cols")
    z, x = r >> 2, r & 3

    def at_x(j):
        return (z * X + ((x + j) & 3), c)

    def at_z(o):
        return (((z + o) & 7) * X + x, c)

    def at_c(k):
        return (r, (c + k) & 7)

    def remote(src, dst, send, recv, dev):
        return pltpu.make_async_remote_copy(
            src_ref=src, dst_ref=dst, send_sem=send, recv_sem=recv,
            device_id=dev, device_id_type=MESH,
        )

    def loop(n, f):
        def step(i, carry):
            f(i)
            return carry

        lax.fori_loop(0, n, step, 0)

    def rows_of(j):
        return pl.ds(pl.multiple_of(((x + j) & 3) * RB, 8), RB)

    def far(k):
        return (z + far_first(k)) & 7

    def near(k):
        return (z + 8 - near_first(k)) & 7

    def load(k):
        columns = pl.ds(pl.multiple_of(far(k) * CH, CH), CH)
        return pltpu.make_async_copy(coupling.at[:, :, columns], stage.at[far(k)], hsem.at[far(k)])

    loop(Z, lambda k: load(k).start())

    barrier = pltpu.get_barrier_semaphore()
    partners = [at_x(j) for j in range(1, X)] + [at_z(o) for o in range(1, Z)]
    partners += [at_c(k) for k in range(1, C)]
    for dev in partners:
        pl.semaphore_signal(barrier, inc=1, device_id=dev, device_id_type=MESH)

    def set_left(re, im):
        top = jnp.concatenate([re, im], axis=1)
        bottom = jnp.concatenate([im, -re], axis=1)
        high, low = split(jnp.concatenate([top, bottom], axis=0))
        lhs[...] = jnp.concatenate([high, low], axis=0)


    def x_part(j, zc):
        return remote(
            part.at[zc, rows_of(j)], rsx.at[j - 1, zc], rsx_s.at[j - 1, zc], rsx_r.at[j - 1, zc], at_x(j)
        )

    def z_part(k):
        o = far_first(k)
        return remote(red.at[far(k)], rsz.at[o], rsz_s.at[o], rsz_r.at[o], at_z(o))

    def send_parts(k):
        for j in (1, 3, 2):
            x_part(j, far(k)).start()

    def whole_part():
        return remote(part.at[far(0)], big, rw_s.at[0], rw_r.at[0], at_z(4))

    def column_product(load_first, send):
        def chunk(k):
            zc = far(k)
            if load_first:
                load(k).wait()
                for t in range(0, 1024, 128):
                    high, low = split(stage[zc, t // 512, t % 512 : t % 512 + 128])
                    hhi[zc, t : t + 128] = high
                    hlo[zc, t : t + 128] = low
            both = dot(lhs[...], hhi[zc])
            part[zc] = both[: 2 * K] + both[2 * K :] + dot(lhs[: 2 * K], hlo[zc])
            if send:

                @pl.when(k == 0)
                def _():
                    whole_part().start()

                @pl.when((k > 0) & (k < Z - 1))
                def _():
                    send_parts(k)

        loop(Z, chunk)

    def column_sum():
        def chunk(i):
            k = i + 1
            zc = far(k)

            @pl.when(k == 5)
            def _():
                whole_part().wait_recv()
                part[z] = part[z] + big[...]
                send_parts(Z - 1)

            total = part[zc, rows_of(0)]
            for j in range(1, X):
                x_part(j, zc).wait_recv()
                total = total + rsx[j - 1, zc]
            red[zc] = total

            @pl.when(k < Z - 1)
            def _():
                z_part(k).start()

        loop(Z - 1, chunk)


    def z_whole(o, zc):
        block = gath.at[zc, rows_of(0)]
        return remote(block, block, agz_s.at[o], agz_r.at[o], at_z(o))

    def x_whole(j, zc, shift):
        block = gath.at[zc, rows_of(shift)]
        return remote(block, block, agx_s.at[j - 1, zc], agx_r.at[j - 1, zc], at_x(j))

    def whole_block(zc):
        return remote(gath.at[zc], gath.at[zc], aw_s.at[0], aw_r.at[0], at_z(4))

    def column_gather(tiles):
        def last(k, total):
            z_part(k).wait_recv()
            return total + rsz[far_first(k)]

        gath[z, rows_of(0)] = lax.fori_loop(1, Z - 1, last, red[z])
        loop(Z - 2, lambda k: z_whole(far_first(k + 1), z).start())
        for j in (1, 3, 2):
            x_whole(j, z, 0).start()

        def forward(k):
            z_whole(near_first(k), near(k)).wait_recv()
            for j in (1, 3, 2):
                x_whole(j, near(k), 0).start()

            @pl.when(k == 2)
            def _():
                for j in range(1, X):
                    x_whole(j, z, X - j).wait_recv()
                whole_block(z).start()

        def step(k, tiles):
            tiles = factor_block(k, tiles)
            forward(k + 1)
            return tiles

        if tiles is None:
            loop(Z - 2, lambda k: forward(k + 1))
            return None
        tiles = lax.fori_loop(0, K // 8, step, tiles)
        return factor_end(tiles)

    def column_sent():
        def chunk(i):
            k = i + 1
            for j in range(1, X):
                x_part(j, far(k)).wait_send()
                x_whole(j, far(k), 0).wait_send()

            @pl.when(k < Z - 1)
            def _():
                z_part(k).wait_send()
                z_whole(far_first(k), z).wait_send()

        loop(Z - 1, chunk)
        whole_part().wait_send()
        whole_block(z).wait_send()

    def c_gram(t, k):
        return remote(gsrc, gyc.at[t, k], gyc_s.at[t, k], gyc_r.at[t, k], at_c(k))

    def c_scatter(t, k):
        return remote(scat.at[t, (c + k) & 7], ypc.at[t], sc_s.at[t, k], sc_r.at[t], at_c(k))

    def c_part(k):
        return remote(pk.at[(c + k) & 7], rsy.at[k], rsy_s.at[k], rsy_r.at[k], at_c(k))

    def row_product(t, factor):
        acc[...] = jnp.zeros_like(acc)
        acc2[...] = jnp.zeros_like(acc2)
        gsum[...] = jnp.zeros_like(gsum)

        def receive(k):
            zc = near(k)

            @pl.when((k > 0) & (k < Z - 1))
            def _():
                for j in range(1, X):
                    x_whole(j, zc, X - j).wait_recv()

            @pl.when(k == Z - 1)
            def _():
                whole_block(zc).wait_recv()

            block = gath[zc]
            if factor is not None:
                block = in_parts(dot, factor, block)
            ybuf[zc] = block
            high, low = split(block)
            acc[...] += dot_nt(jnp.concatenate([high, low], axis=0), hhi[zc])
            acc2[...] += dot_nt(high, hlo[zc])
            gsum[...] += gram_planes(block[:K], block[K:])

        loop(Z, receive)
        total = acc[: 2 * K] + acc[2 * K :] + acc2[...]
        re = total[:K, :512] - total[K:, 512:]
        im = total[K:, :512] + total[:K, 512:]
        for q in range(4):
            even, odd = pack_pair(re[:, 128 * q : 128 * q + 128], im[:, 128 * q : 128 * q + 128])
            pk[2 * q], pk[2 * q + 1] = even, odd
        for k in range(1, C):
            c_part(k).start()

        @pl.when(c == z)
        def _():
            for q in range(4):
                chunk = ybuf.at[2 * x + q // 2]
                part_lanes = slice((q % 2) * 128, (q % 2) * 128 + 128)
                even, odd = pack_pair(chunk[:K, part_lanes], chunk[K:, part_lanes])
                scat[t, 2 * q], scat[t, 2 * q + 1] = even, odd
            for k in range(1, C):
                c_scatter(t, k).start()
            ypc[t] = scat[t, c]

        gsrc[...] = pack_triangle(gsum[...])
        for k in range(1, C):
            c_gram(t, k).start()

    def row_sum():
        total = pk[c]
        for k in range(1, C):
            c_part(k).wait_recv()
            total = total + rsy[k]
        return total

    def c_factor(t):
        total = gsrc[...]
        for k in range(1, C):
            c_gram(t, k).wait_recv()
            total = total + gyc[t, k]
        return inverse_factor(unpack_triangle(total * (1.0 / N)))

    def scattered(t):
        @pl.when(c != z)
        def _():
            c_scatter(t, 1).wait_recv()

        return ypc[t]

    def row_sent(t):
        for k in range(1, C):
            c_part(k).wait_send()
            c_gram(t, k).wait_send()

        @pl.when(c == z)
        def _():
            for k in range(1, C):
                c_scatter(t, k).wait_send()

    def slab(shift):
        return pl.ds(pl.multiple_of(((c + shift) & 7) * RB, 8), RB)

    def p_c(k):
        return remote(psrc.at[slab(k)], py.at[k], py_s.at[k], py_r.at[k], at_c(k))

    def p_x(j):
        return remote(px.at[0], px.at[j], px_s.at[j], px_r.at[j], at_x(j))

    def p_z(o):
        return remote(pz.at[0], pz.at[o], pz_s.at[o], pz_r.at[o], at_z(o))

    def p_all(k, shift):
        return remote(pall.at[slab(shift)], pall.at[slab(shift)], pa_s.at[k], pa_r.at[k], at_c(k))

    def added(total, n, copy, slots):
        for i in range(1, n):
            copy(i).wait_recv()
            total = total + slots[i]
        return total

    v_re, v_im = initial[0], initial[1]
    set_left(v_re, v_im)
    pl.semaphore_wait(barrier, len(partners))
    column_product(True, True)
    for q in range(4):
        even, odd = pack_pair(v_re[:, 128 * q : 128 * q + 128], v_im[:, 128 * q : 128 * q + 128])
        pk[2 * q], pk[2 * q + 1] = even, odd
    v_piece = pk[c]
    column_sum()
    column_gather(None)
    row_product(0, None)
    z2_piece = row_sum()
    gy[c] = z2_piece

    def c_whole(k, src):
        return remote(gy.at[src], gy.at[src], agy_s.at[k], agy_r.at[k], at_c(k))

    for k in range(1, C):
        c_whole(k, c).start()
    inv1 = c_factor(0)
    column_sent()
    for k in range(1, C):
        c_whole(k, (c + C - k) & 7).wait_recv()
    pairs = [unpack_pair(gy[2 * q], gy[2 * q + 1]) for q in range(4)]
    block = jnp.concatenate(
        [jnp.concatenate([pair[p] for pair in pairs], axis=1) for p in range(2)], axis=0
    )
    block = in_parts(dot, embedded(inv1), block)
    set_left(block[:K], block[K:])
    gxs[...] = pack_triangle(gram_planes(block[:K], block[K:]))

    def x_gram(j):
        return remote(gxs, gx.at[j], gx_s.at[j], gx_r.at[j], at_x(j))

    def z_gram(o):
        return remote(gzs, gz.at[o], gz_s.at[o], gz_r.at[o], at_z(o))

    for j in range(1, X):
        x_gram(j).start()
    column_product(False, True)
    total = gxs[...]
    for j in range(1, X):
        x_gram(j).wait_recv()
        total = total + gx[j]
    gzs[...] = total
    for o in range(1, Z):
        z_gram(o).start()
    row_sent(0)
    y2_piece = apply_packed(inv1, z2_piece)
    y1_piece = scattered(0)
    psrc[:K] = gram_packed(v_piece, y1_piece)
    psrc[K : 2 * K] = conj_apply_packed(inv1, gram_packed(y1_piece, y2_piece))
    psrc[2 * K :] = jnp.zeros((2 * K, 128), F32)
    for k in range(1, C):
        p_c(k).start()
    column_sum()
    total = gzs[...]
    for o in range(1, Z):
        z_gram(o).wait_recv()
        total = total + gz[o]
    inv2 = column_gather(factor_start(unpack_triangle(total * (1.0 / N))))
    px[0] = added(psrc[slab(0)], C, p_c, py)
    for j in range(1, X):
        p_x(j).start()
    row_product(1, embedded(inv2))
    pz[0] = added(px[0], X, p_x, px)
    for o in range(1, Z):
        p_z(o).start()
    z4_piece = row_sum()


    def g_c(m, k):
        return remote(g4.at[m, 0], g4y.at[m, k], g4y_s.at[m, k], g4y_r.at[m, k], at_c(k))

    def g_x(m, j):
        return remote(g4.at[m, 1], g4x.at[m, j], g4x_s.at[m, j], g4x_r.at[m, j], at_x(j))

    def g_z(m, o):
        return remote(g4.at[m, 2], g4z.at[m, o], g4z_s.at[m, o], g4z_r.at[m, o], at_z(o))

    def last_start(m, total):
        g4[m, 0] = total
        for k in range(1, C):
            g_c(m, k).start()
        return total

    def last_x(m, total):
        for k in range(1, C):
            g_c(m, k).wait_recv()
            total = total + g4y[m, k]
        g4[m, 1] = total
        for j in range(1, X):
            g_x(m, j).start()
        return total

    def last_z(m, total):
        for j in range(1, X):
            g_x(m, j).wait_recv()
            total = total + g4x[m, j]
        g4[m, 2] = total
        for o in range(1, Z):
            g_z(m, o).start()
        return total

    def last_end(m, total):
        for o in range(1, Z):
            g_z(m, o).wait_recv()
            total = total + g4z[m, o]
        return unpack_triangle(total * (1.0 / N))

    gram = last_start(0, pack_triangle(gram_packed(z4_piece, z4_piece)))
    y3_piece = scattered(1)
    projection = last_start(1, pack_triangle(gram_packed(y3_piece, z4_piece)))
    third = last_start(2, pack_triangle(conj_apply_packed(inv2, gram_packed(y2_piece, y3_piece))))
    inv3 = c_factor(1)
    gram = last_x(0, gram)
    y4_piece = apply_packed(inv3, z4_piece)
    projection = last_x(1, projection)
    third = last_x(2, third)
    gram = last_z(0, gram)
    pall[slab(0)] = added(pz[0], Z, p_z, pz) * (1.0 / N)
    for k in range(1, C):
        p_all(k, 0).start()
    projection = last_z(1, projection)
    third = last_z(2, third)
    column_sent()
    row_sent(1)
    for k in range(1, C):
        c_whole(k, c).wait_send()
        for m in range(3):
            g_c(m, k).wait_send()
        p_c(k).wait_send()
    for j in range(1, X):
        x_gram(j).wait_send()
        for m in range(3):
            g_x(m, j).wait_send()
        p_x(j).wait_send()
    for o in range(1, Z):
        z_gram(o).wait_send()
    gram = both_sides(inv3, last_end(0, gram))
    last_value[...] = apply_packed(inverse_factor(gram), y4_piece)
    last_projections[3 * K :] = both_sides(inv3, last_end(1, projection))
    for k in range(1, C):
        p_all(k, C - k).wait_recv()
    last_projections[: 2 * K] = pall[: 2 * K]
    last_projections[2 * K : 3 * K] = last_end(2, third)

    for k in range(1, C):
        p_all(k, 0).wait_send()
    for o in range(1, Z):
        for m in range(3):
            g_z(m, o).wait_send()
        p_z(o).wait_send()


def solution(mesh):
    dma = pltpu.SemaphoreType.DMA
    packed, piece = (K, 128), (RB, 128)
    scratch = [
        pltpu.VMEM((Z, 2, 512, CH), F32),
        pltpu.VMEM((Z, 1024, CH), BF16),
        pltpu.VMEM((Z, 1024, CH), BF16),
        pltpu.VMEM((4 * K, 1024), BF16),
        pltpu.VMEM((Z, 2 * K, CH), F32),
        pltpu.VMEM((3, Z, RB, CH), F32),
        pltpu.VMEM((Z, RB, CH), F32),
        pltpu.VMEM((Z, RB, CH), F32),
        pltpu.VMEM((Z, 2 * K, CH), F32),
        pltpu.VMEM((Z, 2 * K, CH), F32),
        pltpu.VMEM((4 * K, 1024), F32),
        pltpu.VMEM((2 * K, 1024), F32),
        pltpu.VMEM((C, *packed), F32),
        pltpu.VMEM((C, *packed), F32),
        pltpu.VMEM((C, *packed), F32),
        pltpu.VMEM((2, C, *packed), F32),
        pltpu.VMEM((2, *packed), F32),
        pltpu.VMEM(packed, F32),
        pltpu.VMEM(piece, F32),
        pltpu.VMEM((2, C, *piece), F32),
        pltpu.VMEM(piece, F32),
        pltpu.VMEM((X, *piece), F32),
        pltpu.VMEM(piece, F32),
        pltpu.VMEM((Z, *piece), F32),
        pltpu.VMEM((3, 3, *piece), F32),
        pltpu.VMEM((3, C, *piece), F32),
        pltpu.VMEM((3, X, *piece), F32),
        pltpu.VMEM((3, Z, *piece), F32),
        pltpu.VMEM((4 * K, 128), F32),
        pltpu.VMEM((C, *piece), F32),
        pltpu.VMEM((X, *piece), F32),
        pltpu.VMEM((Z, *piece), F32),
        pltpu.VMEM((4 * K, 128), F32),
        dma((Z,)),
        pltpu.VMEM((2 * K, CH), F32),
        dma((1,)), dma((1,)), dma((1,)), dma((1,)),
        dma((3, Z)), dma((3, Z)), dma((Z,)), dma((Z,)),
        dma((Z,)), dma((Z,)), dma((3, Z)), dma((3, Z)),
        dma((C,)), dma((C,)), dma((C,)), dma((C,)),
        dma((2, C)), dma((2,)), dma((2, C)), dma((2, C)),
        dma((X,)), dma((X,)), dma((Z,)), dma((Z,)),
        dma((3, C)), dma((3, C)), dma((3, X)), dma((3, X)), dma((3, Z)), dma((3, Z)),
        dma((C,)), dma((C,)), dma((X,)), dma((X,)), dma((Z,)), dma((Z,)), dma((C,)), dma((C,)),
    ]
    vmem = pl.BlockSpec(memory_space=pltpu.VMEM)

    def body(coupling, initial):
        value, projections = pl.pallas_call(
            kernel,
            name="subspace",
            out_shape=(
                jax.ShapeDtypeStruct((K, 128), F32),
                jax.ShapeDtypeStruct((ITERS * K, 128), F32),
            ),
            in_specs=[pl.BlockSpec(memory_space=pl.ANY), vmem],
            out_specs=(vmem, vmem),
            scratch_shapes=scratch,
            compiler_params=pltpu.CompilerParams(
                collective_id=0, has_side_effects=True, vmem_limit_bytes=56 * 1024 * 1024
            ),
        )(coupling, initial)
        return pl.pallas_call(
            results_kernel,
            name="results",
            out_shape=(
                jax.ShapeDtypeStruct((2, K, 64), F32),
                jax.ShapeDtypeStruct((ITERS, 2, K, K), F32),
            ),
            in_specs=[vmem, vmem],
            out_specs=(vmem, vmem),
        )(value, projections)

    return jax.shard_map(
        body,
        mesh=mesh,
        in_specs=(P(None, "rows", "cols"), P(None, None, "rows")),
        out_specs=(P(None, None, ("rows", "cols")), P()),
        check_vma=False,
    )
```
